32 devices in a mesh: blk: 16 (over z, y, x), mp: 2 (over core).
Axes of the slice: x: 2, y: 2, z: 4, core: 2. Of those that a mesh axis runs over, the one named last changes fastest.
Arguments:
- queries: bfloat16 [4096, 5120], P('blk', 'mp'), may hold values from -8.5 to 8.5
- suffix_key_rows: bfloat16 [4096, 1024], P('blk', 'mp'), may hold values from -6 to 6
- suffix_value_rows: bfloat16 [4096, 1024], P('blk', 'mp'), may hold values from -6 to 6
- shared_prefix_keys: bfloat16 [512, 1024], P('blk', 'mp'), may hold values from -8.5 to 8.5
- shared_prefix_values: bfloat16 [512, 1024], P('blk', 'mp'), may hold values from -6 to 6
- out_weight: bfloat16 [5120, 5120], P('mp', 'blk'), may hold values from -0.078125 to 0.078125
- lengths: int32 [16], replicated, may hold values from 1 to 1024, 4096 in all
Outputs:
- output: bfloat16 [4096, 5120], P('blk', 'mp')
The draws below stay inside these ranges and needn't reach their ends.
Inputs may be any that keep to these rules, and one draw needn't show every extreme that they name: The lengths sum to 4096; the longest is exactly 1024.
All inputs are finite; a program needn't handle non-finite values.
Results may differ from the reference program's by a relative error of at most 0.019.
Values may be sent and summed in bfloat16 or wider, within the bound.
A program may use at most 64 MiB of HBM per device.

```python
import math
import jax
import jax.numpy as jnp
import numpy as np
from jax import lax

D = 5120
QUERY_HEADS = 40
KEY_VALUE_HEADS = 8
HEAD_SIZE = 128
REQS = 16
SUF_DEV = 256
SUFFIX_TOKENS = 4096
PREFIX_TOKENS = 512
LONGEST_SUFFIX = 1024
N_MP = 2


def pair_base(key):
    base_key = jax.random.fold_in(key, 11)
    key_query, prefix_key_slice = jax.random.split(base_key)
    query_base = jnp.clip(jax.random.normal(key_query, (SUFFIX_TOKENS, QUERY_HEADS * HEAD_SIZE), jnp.float32), -6.0, 6.0)
    prefix_start_index = jnp.clip(jax.random.normal(prefix_key_slice, (PREFIX_TOKENS, KEY_VALUE_HEADS * HEAD_SIZE), jnp.float32), -6.0, 6.0)
    return (query_base, prefix_start_index)


def draw_shared_prefix_keys(key, part):
    query_base, prefix_start_index = pair_base(key)
    return prefix_start_index.astype(jnp.bfloat16)


def draw_queries(key, part):
    query_base, prefix_start_index = pair_base(key)
    return query_base.astype(jnp.bfloat16)


def block_scale(own_key, shape, pieces, low, largest):
    def one(position, parts):
        draws = jax.random.uniform(jax.random.fold_in(jax.random.fold_in(own_key, 6), position), (parts,), jnp.float32, low / len(pieces), largest / len(pieces))
        return jnp.repeat(jnp.exp(draws), shape[position] // parts).reshape((-1,) + (1,) * (len(shape) - position - 1))

    factor_of = one(*pieces[0])
    for cut in pieces[1:]:
        factor_of = factor_of * one(*cut)
    return factor_of


def length_profile(amount, total, most, lean):
    loads = [(1 << 20) // math.isqrt(standing ** lean) + 1 for standing in range(2, amount + 1)]
    rest, counts = total - most - (amount - 1), [1] * (amount - 1)
    while rest > 0:
        movable = [i for i in range(amount - 1) if counts[i] < most]
        pool, budget = sum([loads[i] for i in movable]), rest
        for i in movable:
            more = min(most - counts[i], max(1, budget * loads[i] // pool), rest)
            counts[i] = counts[i] + more
            rest = rest - more
    return np.array([most] + counts)


def uneven(stream_key, amount, total, limit, slope):
    if amount == 2:
        one = jax.random.randint(stream_key, (), max(1, total - limit), min(limit, total - 1) + 1)
        return jnp.stack([one, total - one])
    sizes = jnp.asarray(length_profile(amount, total, limit, slope), jnp.int32)
    twos = (amount - 1) // 2
    donor, sink = sizes[1:1 + 2 * twos:2], sizes[2:2 + 2 * twos:2]
    room = jnp.minimum(donor - 1, limit - sink)
    shifted = jax.random.randint(jax.random.fold_in(stream_key, 1), (twos,), 0, 1 << 20) % (room + 1)
    sizes = sizes.at[1:1 + 2 * twos:2].set(donor - shifted).at[2:2 + 2 * twos:2].set(sink + shifted)
    return sizes[jax.random.permutation(jax.random.fold_in(stream_key, 2), amount)]


def gaussian(rng, extent, deviation, reach, cuts=(), held_as=jnp.bfloat16):
    drawn = jax.random.normal(rng, extent, jnp.float32) * deviation
    if len(cuts) > 0:
        drawn = block_scale(rng, extent, cuts, -0.22, 0.18) * drawn
    return jnp.clip(drawn, min=-reach, max=reach).astype(held_as)


def setup_inputs(seed: int = 0) -> dict:
    arg_keys = jax.random.split(jax.random.key(seed), 8)
    queries = draw_queries(jax.random.fold_in(arg_keys[7], 71), 0)
    suffix_key_rows = gaussian(arg_keys[1], (SUFFIX_TOKENS, KEY_VALUE_HEADS * HEAD_SIZE), 1.0, 6.0, ((0, 16), (1, 2)))
    suffix_value_rows = gaussian(arg_keys[2], (SUFFIX_TOKENS, KEY_VALUE_HEADS * HEAD_SIZE), 1.0, 6.0, ((0, 16), (1, 2)))
    shared_prefix_keys = draw_shared_prefix_keys(jax.random.fold_in(arg_keys[7], 71), 0)
    shared_prefix_values = gaussian(arg_keys[4], (PREFIX_TOKENS, KEY_VALUE_HEADS * HEAD_SIZE), 1.0, 6.0, ((0, 16), (1, 2)))
    out_weight = gaussian(arg_keys[5], (QUERY_HEADS * HEAD_SIZE, D), (QUERY_HEADS * HEAD_SIZE) ** -0.5, 0.078125, ((0, 2), (1, 16)))
    lengths = uneven(arg_keys[6], REQS, SUFFIX_TOKENS, LONGEST_SUFFIX, 2).astype(jnp.int32)
    return {"queries": queries, "suffix_key_rows": suffix_key_rows, "suffix_value_rows": suffix_value_rows, "shared_prefix_keys": shared_prefix_keys, "shared_prefix_values": shared_prefix_values, "out_weight": out_weight, "lengths": lengths}


MASKED_SCORE = -1e+30

def reference(queries, suffix_key_rows, suffix_value_rows, shared_prefix_keys, shared_prefix_values, out_weight, lengths):
    heads_per_group = QUERY_HEADS // KEY_VALUE_HEADS
    score_scale = 1.0 / math.sqrt(HEAD_SIZE)
    req_ends = jnp.cumsum(lengths).astype(jnp.int32)
    positions = jnp.arange(SUFFIX_TOKENS, dtype=jnp.int32)
    owners = lax.optimization_barrier(jnp.sum((positions[:, None] >= req_ends[None, :]).astype(jnp.int32), axis=1)).astype(jnp.int32)
    rows_per_block = SUF_DEV
    visible_window = LONGEST_SUFFIX + rows_per_block
    padded_keys = jnp.concatenate([jnp.zeros((LONGEST_SUFFIX, KEY_VALUE_HEADS * HEAD_SIZE), jnp.bfloat16), suffix_key_rows], axis=0)
    padded_values = jnp.concatenate([jnp.zeros((LONGEST_SUFFIX, KEY_VALUE_HEADS * HEAD_SIZE), jnp.bfloat16), suffix_value_rows], axis=0)
    pad_owners = jnp.concatenate([jnp.full((LONGEST_SUFFIX,), -1, jnp.int32), owners], axis=0)
    prefix_key_rows = shared_prefix_keys.astype(jnp.float32).reshape(PREFIX_TOKENS, KEY_VALUE_HEADS, HEAD_SIZE)
    prefix_value_rows = shared_prefix_values.astype(jnp.float32).reshape(PREFIX_TOKENS, KEY_VALUE_HEADS, HEAD_SIZE)

    def one_block(start_index):
        start_index = start_index.astype(jnp.int32)
        query_row_slice = lax.dynamic_slice_in_dim(queries, start_index, rows_per_block, 0)
        heads_of_query = query_row_slice.astype(jnp.float32).reshape(rows_per_block, KEY_VALUE_HEADS, heads_per_group, HEAD_SIZE)
        key_row_slice = lax.dynamic_slice_in_dim(padded_keys, start_index, visible_window, 0).astype(jnp.float32).reshape(visible_window, KEY_VALUE_HEADS, HEAD_SIZE)
        value_row_slice = lax.dynamic_slice_in_dim(padded_values, start_index, visible_window, 0).astype(jnp.float32).reshape(visible_window, KEY_VALUE_HEADS, HEAD_SIZE)
        key_owner = lax.dynamic_slice_in_dim(pad_owners, start_index, visible_window, 0)
        query_owner = lax.dynamic_slice_in_dim(owners, start_index, rows_per_block, 0)
        key_pos = start_index - LONGEST_SUFFIX + jnp.arange(visible_window, dtype=jnp.int32)
        query_pos = start_index + jnp.arange(rows_per_block, dtype=jnp.int32)
        visible = (key_owner[None, :] == query_owner[:, None]) & (key_pos[None, :] <= query_pos[:, None]) & (key_pos[None, :] >= 0)
        pre_scores = jnp.einsum('qhgd,khd->hgqk', heads_of_query, prefix_key_rows) * score_scale
        suf_scores = jnp.einsum('qhgd,khd->hgqk', heads_of_query, key_row_slice) * score_scale
        suf_scores = jnp.where(visible[None, None], suf_scores, MASKED_SCORE)
        peak = jnp.maximum(lax.optimization_barrier(jnp.max(pre_scores, axis=-1)), lax.optimization_barrier(jnp.max(suf_scores, axis=-1)))
        pre_weights = jnp.exp(pre_scores - peak[..., None])
        suf_weights = jnp.where(visible[None, None], jnp.exp(suf_scores - peak[..., None]), 0.0)
        total = lax.optimization_barrier(jnp.sum(pre_weights, axis=-1)) + lax.optimization_barrier(jnp.sum(suf_weights, axis=-1))
        pre_low = lax.optimization_barrier(pre_weights.astype(jnp.bfloat16)).astype(jnp.float32)
        suf_low = lax.optimization_barrier(suf_weights.astype(jnp.bfloat16)).astype(jnp.float32)
        summed = jnp.einsum('hgqk,khd->hgqd', pre_low, prefix_value_rows) + jnp.einsum('hgqk,khd->hgqd', suf_low, value_row_slice)
        attended = summed / total[..., None]
        return jnp.transpose(attended, (2, 0, 1, 3)).reshape(rows_per_block, QUERY_HEADS * HEAD_SIZE).astype(jnp.bfloat16)
    starts = jnp.arange(SUFFIX_TOKENS // rows_per_block, dtype=jnp.int32) * rows_per_block
    attn = lax.map(one_block, starts).reshape(SUFFIX_TOKENS, QUERY_HEADS * HEAD_SIZE)
    group_cols = QUERY_HEADS * HEAD_SIZE // N_MP
    summed_out = jnp.zeros((SUFFIX_TOKENS, D), jnp.float32)
    for group_index in range(N_MP):
        attn_cols = attn[:, group_index * group_cols:(group_index + 1) * group_cols]
        weight_rows = out_weight[group_index * group_cols:(group_index + 1) * group_cols]
        partial_value = jnp.dot(attn_cols, weight_rows, preferred_element_type=jnp.float32)
        partial_value = lax.optimization_barrier(partial_value.astype(jnp.bfloat16)).astype(jnp.float32)
        summed_out = summed_out + partial_value
    return summed_out.astype(jnp.bfloat16)
```

```python
import math

import jax
import jax.numpy as jnp
from jax import lax
from jax.experimental import pallas as pl
from jax.experimental.pallas import tpu as pltpu
from jax.sharding import PartitionSpec as P

HEAD_SIZE = 128


MASKED_SCORE = -1e30


def passed_along(block, axis, distance):
    devices = range(lax.axis_size(axis))
    route = [(i - distance, i) for i in devices if i - distance in devices]
    return lax.ppermute(block, axis, route)


def per_device(
    queries,
    suffix_key_rows,
    suffix_value_rows,
    shared_prefix_keys,
    shared_prefix_values,
    out_weight,
    lengths,
):
    tok_rows = queries.shape[0]
    kv_heads = suffix_key_rows.shape[1] // HEAD_SIZE
    q_heads = queries.shape[1] // HEAD_SIZE
    heads_per_group = q_heads // kv_heads
    blocks = lax.axis_size("blk")
    cycle_reach = blocks // 4
    my_block = lax.axis_index("blk")
    score_scale = 1.0 / math.sqrt(HEAD_SIZE)
    heads_of_query = queries.reshape(tok_rows, kv_heads, heads_per_group, HEAD_SIZE)
    req_ends = jnp.cumsum(lengths)
    local_rows = jnp.arange(tok_rows, dtype=jnp.int32)
    query_pos = my_block * tok_rows + local_rows

    def owner_of(position):
        return jnp.sum((position[:, None] >= req_ends[None, :]).astype(jnp.int32), axis=1)

    query_owner = owner_of(query_pos)

    def update(carry_state, key_block, value_block, visible):
        run_max, row_total, accumulated = carry_state
        count = key_block.shape[0]
        key_heads = key_block.reshape(count, kv_heads, HEAD_SIZE)
        value_heads = value_block.reshape(count, kv_heads, HEAD_SIZE)
        scores = (
            jnp.einsum(
                "qhgd,khd->hgqk", heads_of_query, key_heads, preferred_element_type=jnp.float32
            )
            * score_scale
        )
        if visible is not None:
            scores = jnp.where(visible[None, None], scores, MASKED_SCORE)
        new_max = jnp.maximum(run_max, jnp.max(scores, axis=-1))
        weights = jnp.exp(scores - new_max[..., None])
        if visible is not None:
            weights = jnp.where(visible[None, None], weights, 0.0)
        rescale = jnp.exp(run_max - new_max)
        row_total = row_total * rescale + jnp.sum(weights, axis=-1)
        contrib = jnp.einsum(
            "hgqk,khd->hgqd",
            weights.astype(jnp.bfloat16),
            value_heads,
            preferred_element_type=jnp.float32,
        )
        accumulated = accumulated * rescale[..., None] + contrib
        return (new_max, row_total, accumulated)

    start_state = (
        jnp.full((kv_heads, heads_per_group, tok_rows), MASKED_SCORE, jnp.float32),
        jnp.zeros((kv_heads, heads_per_group, tok_rows), jnp.float32),
        jnp.zeros((kv_heads, heads_per_group, tok_rows, HEAD_SIZE), jnp.float32),
    )
    carry_state = update(
        start_state,
        lax.all_gather(shared_prefix_keys, "blk", axis=0, tiled=True),
        lax.all_gather(shared_prefix_values, "blk", axis=0, tiled=True),
        None,
    )

    def visible_from(distance):
        key_pos = (my_block - distance) * tok_rows + local_rows
        key_owner = owner_of(key_pos)
        return (
            (key_owner[None, :] == query_owner[:, None])
            & (key_pos[None, :] <= query_pos[:, None])
            & (key_pos[None, :] >= 0)
        )

    kv_pair = jnp.stack((suffix_key_rows, suffix_value_rows))
    carry_state = update(carry_state, kv_pair[0], kv_pair[1], visible_from(0))

    def advance(distance, loop_carry):
        current, moving = loop_carry
        moving = passed_along(moving, "blk", 1)
        visible = visible_from(distance)
        current = update(current, moving[0], moving[1], visible)
        return (current, moving)

    carry_state, kv_pair = lax.fori_loop(1, cycle_reach + 1, advance, (carry_state, kv_pair))
    run_max, row_total, accumulated = carry_state
    attended = accumulated / row_total[..., None]
    attn = (
        jnp.transpose(attended, (2, 0, 1, 3))
        .reshape(tok_rows, q_heads * HEAD_SIZE)
        .astype(jnp.bfloat16)
    )
    product = jnp.dot(
        attn,
        lax.all_gather(out_weight, "blk", axis=1, tiled=True),
        preferred_element_type=jnp.float32,
    )
    return lax.psum_scatter(product.astype(jnp.bfloat16), "mp", scatter_dimension=1, tiled=True)


MESH = pl.DeviceIdType.MESH
NT = (((1,), (1,)), ((), ()))
REACH = 4
PLANE = 4


def fused_kernel(
    q_ref, k_ref, v_ref, pk_ref, pv_ref, w_ref, len_ref,
    out_ref,
    keys, values, bias, weights, attn, mine, to_core, from_core, summed,
    pz_s, pz_r, pp_s, pp_r, sx_s, sx_r, w_s, w_r, at_s, at_r, mp_s, mp_r, out_s, out_r,
):
    rows = q_ref.shape[0]
    kv_heads = k_ref.shape[1] // HEAD_SIZE
    group = q_ref.shape[1] // k_ref.shape[1]
    part = pk_ref.shape[0]
    prefix = part * PLANE * PLANE
    chunk = part * PLANE
    me = lax.axis_index("blk")
    mp = lax.axis_index("mp")
    z = lax.div(me, PLANE)
    i = lax.rem(me, PLANE)

    def send(src, dst, send_sem, recv_sem, blk, core=None):
        return pltpu.make_async_remote_copy(
            src_ref=src, dst_ref=dst, send_sem=send_sem, recv_sem=recv_sem,
            device_id=(blk, mp if core is None else core), device_id_type=MESH,
        )

    def in_column(o):
        return lax.rem(z + o, PLANE) * PLANE + i

    def in_plane(o):
        return z * PLANE + lax.rem(i + o, PLANE)

    barrier = pltpu.get_barrier_semaphore()
    for o in (1, 2, 3):
        pl.semaphore_signal(barrier, inc=1, device_id=(in_column(o), mp), device_id_type=MESH)
        pl.semaphore_signal(barrier, inc=1, device_id=(in_plane(o), mp), device_id_type=MESH)
    pl.semaphore_signal(barrier, inc=1, device_id=(me, 1 - mp), device_id_type=MESH)
    pl.semaphore_wait(barrier, 7)

    kv = ((k_ref, pk_ref, keys), (v_ref, pv_ref, values))

    def suffix_rows(d):
        return pl.ds(prefix + d * rows, rows)

    def up_copy(c):
        own, _, held = kv[c]
        return send(own, held.at[suffix_rows(REACH)], sx_s.at[REACH, c], sx_r.at[REACH, c],
                    me + REACH)

    own_rows = pl.ds(pl.multiple_of(i * chunk + z * part, part), part)

    def prefix_up(o, c):
        _, own, held = kv[c]
        return send(own, held.at[own_rows], pz_s.at[o, c], pz_r.at[o, c], in_column(o))

    my_chunk = pl.ds(pl.multiple_of(i * chunk, chunk), chunk)

    def prefix_across(o, c):
        held = kv[c][2]
        return send(held.at[my_chunk], held.at[my_chunk], pp_s.at[o, c], pp_r.at[o, c],
                    in_plane(o))

    def across_own(d, c):
        own, _, held = kv[c]
        return send(own, held.at[suffix_rows(d)], sx_s.at[d, c], sx_r.at[d, c], in_plane(d))

    def across_relayed(d, c):
        held = kv[c][2]
        return send(held.at[suffix_rows(REACH)], held.at[suffix_rows(d)], sx_s.at[d, c],
                    sx_r.at[d, c], in_plane(d))

    def weight_hop(way, k):
        origin = z - (k - 1) if way == 0 else z + (k - 1)
        to = me + PLANE if way == 0 else me - PLANE
        source = w_ref if k == 1 else weights.at[origin]
        return send(source, weights.at[origin], w_s.at[way, k], w_r.at[way, k], to)

    def sends_hop(way, k):
        if way == 0:
            return (z - (k - 1) >= 0) & (z + 1 < PLANE)
        return (z + (k - 1) < PLANE) & (z >= 1)

    def gets_hop(way, k):
        return z - k >= 0 if way == 0 else z + k < PLANE

    def start_hop(k):
        for way in (0, 1):
            @pl.when(sends_hop(way, k))
            def _():
                weight_hop(way, k).start()

    def take_hop(k):
        for way in (0, 1):
            @pl.when(gets_hop(way, k))
            def _():
                weight_hop(way, k).wait_recv()

    for o in (1, 2, 3):
        for c in (0, 1):
            prefix_up(o, c).start()

    @pl.when(z + 1 < PLANE)
    def _():
        up_copy(0).start()
        up_copy(1).start()

    for d in (1, 2, 3):
        @pl.when(i + d < PLANE)
        def _():
            across_own(d, 0).start()
            across_own(d, 1).start()

    start_hop(1)

    keys[own_rows, :] = pk_ref[...]
    values[own_rows, :] = pv_ref[...]
    keys[pl.ds(prefix, rows), :] = k_ref[...]
    values[pl.ds(prefix, rows), :] = v_ref[...]
    weights[z] = w_ref[...]
    for d in range(1, REACH + 1):
        @pl.when(me < d)
        def _():
            keys[suffix_rows(d), :] = jnp.zeros((rows, keys.shape[1]), keys.dtype)
            values[suffix_rows(d), :] = jnp.zeros((rows, keys.shape[1]), keys.dtype)

    query_pos = me * rows + lax.broadcasted_iota(jnp.int32, (rows, HEAD_SIZE), 0)
    first = jnp.zeros((rows, HEAD_SIZE), jnp.int32)
    end = jnp.int32(0)
    for r in range(len_ref.shape[0]):
        end = end + len_ref[r]
        first = jnp.maximum(first, jnp.where(query_pos >= end, end, 0))
    lane = lax.broadcasted_iota(jnp.int32, (rows, HEAD_SIZE), 1)
    for d in range(REACH + 1):
        for t in range(rows // HEAD_SIZE):
            key_pos = (me - d) * rows + t * HEAD_SIZE + lane
            seen = (key_pos >= first) & (key_pos <= query_pos)
            at = d * rows + t * HEAD_SIZE
            bias[:, at:at + HEAD_SIZE] = jnp.where(seen, 0.0, MASKED_SCORE)

    for o in (1, 2, 3):
        for c in (0, 1):
            prefix_up(o, c).wait_recv()
    for o in (1, 2, 3):
        for c in (0, 1):
            prefix_across(o, c).start()

    @pl.when(z >= 1)
    def _():
        up_copy(0).wait_recv()
        up_copy(1).wait_recv()
        for d in (1, 2, 3):
            @pl.when(i + d >= PLANE)
            def _():
                across_relayed(d, 0).start()
                across_relayed(d, 1).start()

    for o in (1, 2, 3):
        for c in (0, 1):
            prefix_across(o, c).wait_recv()
    for d in (1, 2, 3):
        @pl.when(me >= d)
        def _():
            across_own(d, 0).wait_recv()
            across_own(d, 1).wait_recv()

    exponent_scale = math.log2(math.e) / math.sqrt(HEAD_SIZE)
    width = group * HEAD_SIZE

    def attn_part(g, o):
        columns = pl.ds(pl.multiple_of(g * width, HEAD_SIZE), width)
        block = attn.at[i, :, columns]
        return send(block, block, at_s.at[g, o], at_r.at[g, o], in_plane(o))

    def one_group(g, carry):
        head = pl.ds(pl.multiple_of(g * HEAD_SIZE, HEAD_SIZE), HEAD_SIZE)
        for h in range(group):
            column = pl.ds(pl.multiple_of(g * width + h * HEAD_SIZE, HEAD_SIZE), HEAD_SIZE)
            q = q_ref[:, column]
            s_pre = lax.dot_general(q, keys[:prefix, head], NT, preferred_element_type=jnp.float32)
            s_suf = lax.dot_general(q, keys[prefix:, head], NT, preferred_element_type=jnp.float32)
            s_suf = s_suf + bias[...]
            peak = jnp.maximum(
                jnp.max(s_pre, axis=1, keepdims=True), jnp.max(s_suf, axis=1, keepdims=True)
            )
            p_pre = jnp.exp2((s_pre - peak) * exponent_scale)
            p_suf = jnp.exp2((s_suf - peak) * exponent_scale)
            total = jnp.sum(p_pre, axis=1, keepdims=True) + jnp.sum(p_suf, axis=1, keepdims=True)
            mixed = jnp.dot(
                p_pre.astype(jnp.bfloat16), values[:prefix, head],
                preferred_element_type=jnp.float32,
            ) + jnp.dot(
                p_suf.astype(jnp.bfloat16), values[prefix:, head],
                preferred_element_type=jnp.float32,
            )
            attn[i, :, column] = (mixed / total).astype(jnp.bfloat16)
        for o in (1, 2, 3):
            attn_part(g, o).start()

        @pl.when(g == 1)
        def _():
            take_hop(1)
            start_hop(2)

        return carry

    lax.fori_loop(0, kv_heads, one_group, 0)

    take_hop(2)
    start_hop(3)

    def take_attn(g, carry):
        for o in (1, 2, 3):
            attn_part(g, o).wait_recv()
        return carry

    lax.fori_loop(0, kv_heads, take_attn, 0)

    def to_sibling(low, t):
        return send(to_core.at[low, t], from_core.at[low, t], mp_s.at[low, t], mp_r.at[low, t],
                    me, 1 - mp)

    def to_owner(low, t):
        return send(summed.at[low, t], out_ref.at[low * PLANE + i], out_s.at[low, t],
                    out_r.at[low, i], z * PLANE + t)

    def out_arrival(low, t):
        return send(summed.at[low, t], out_ref.at[low * PLANE + t], out_s.at[low, t],
                    out_r.at[low, t], z * PLANE + t)

    def one_shard(n, carry):
        inner = lax.div(z * (3 - z), 2)
        f = n + inner * (1 - 2 * n) * (1 - lax.div(n, 2))
        src = f + lax.div(z, 2) * (3 - 2 * f)
        low = lax.rem(src, 2)
        ours = lax.div(src, 2) == mp

        @pl.when(n == 3)
        def _():
            take_hop(3)

        def one_block(t, c):
            product = lax.dot_general(
                attn[t], weights[src], NT, preferred_element_type=jnp.float32
            ).astype(jnp.bfloat16)

            @pl.when(ours)
            def _():
                mine[t] = product

            @pl.when(jnp.logical_not(ours))
            def _():
                to_core[low, t] = product
                to_sibling(low, t).start()

            return c

        lax.fori_loop(0, PLANE, one_block, 0)

        @pl.when(ours)
        def _():
            def add_block(t, c):
                to_sibling(low, t).wait_recv()
                both = mine[t].astype(jnp.float32) + from_core[low, t].astype(jnp.float32)
                both = both.astype(jnp.bfloat16)

                @pl.when(t == i)
                def _():
                    out_ref[low * PLANE + i] = both

                @pl.when(t != i)
                def _():
                    summed[low, t] = both
                    to_owner(low, t).start()

                return c

            lax.fori_loop(0, PLANE, add_block, 0)

        return carry

    lax.fori_loop(0, PLANE, one_shard, 0)

    for low in (0, 1):
        for t in range(PLANE):
            to_sibling(low, t).wait_send()

            @pl.when(t != i)
            def _():
                out_arrival(low, t).wait_recv()
                out_arrival(low, t).wait_send()

    for o in (1, 2, 3):
        for c in (0, 1):
            prefix_up(o, c).wait_send()
            prefix_across(o, c).wait_send()
            across_own_sent = across_own(o, c)

            @pl.when((i + o < PLANE) | (z >= 1))
            def _():
                across_own_sent.wait_send()
        for g in range(kv_heads):
            attn_part(g, o).wait_send()
    for c in (0, 1):
        @pl.when(z + 1 < PLANE)
        def _():
            up_copy(c).wait_send()
    for k in (1, 2, 3):
        for way in (0, 1):
            @pl.when(sends_hop(way, k))
            def _():
                weight_hop(way, k).wait_send()


def per_device_fused(
    queries,
    suffix_key_rows,
    suffix_value_rows,
    shared_prefix_keys,
    shared_prefix_values,
    out_weight,
    lengths,
):
    rows, q_cols = queries.shape
    kv_cols = suffix_key_rows.shape[1]
    columns = out_weight.shape[1]
    held = shared_prefix_keys.shape[0] * PLANE * PLANE + (REACH + 1) * rows
    kv_heads = kv_cols // HEAD_SIZE
    vmem = pl.BlockSpec(memory_space=pltpu.VMEM)
    low = jnp.bfloat16
    sem = pltpu.SemaphoreType.DMA
    blocks = pl.pallas_call(
        fused_kernel,
        out_shape=jax.ShapeDtypeStruct((2 * PLANE, rows, columns), low),
        in_specs=[vmem] * 6 + [pl.BlockSpec(memory_space=pltpu.SMEM)],
        out_specs=vmem,
        scratch_shapes=[
            pltpu.VMEM((held, kv_cols), low),
            pltpu.VMEM((held, kv_cols), low),
            pltpu.VMEM((rows, (REACH + 1) * rows), jnp.float32),
            pltpu.VMEM((PLANE, columns, q_cols), low),
            pltpu.VMEM((PLANE, rows, q_cols), low),
            pltpu.VMEM((PLANE, rows, columns), low),
            pltpu.VMEM((2, PLANE, rows, columns), low),
            pltpu.VMEM((2, PLANE, rows, columns), low),
            pltpu.VMEM((2, PLANE, rows, columns), low),
            sem((4, 2)), sem((4, 2)), sem((4, 2)), sem((4, 2)),
            sem((REACH + 1, 2)), sem((REACH + 1, 2)),
            sem((2, 4)), sem((2, 4)),
            sem((kv_heads, 4)), sem((kv_heads, 4)),
            sem((2, PLANE)), sem((2, PLANE)), sem((2, PLANE)), sem((2, PLANE)),
        ],
        compiler_params=pltpu.CompilerParams(
            collective_id=0, has_side_effects=True, vmem_limit_bytes=52 * 1024 * 1024
        ),
        cost_estimate=pl.CostEstimate(
            flops=12_000_000_000, bytes_accessed=8_000_000, transcendentals=10_000_000
        ),
    )(
        queries, suffix_key_rows, suffix_value_rows, shared_prefix_keys, shared_prefix_values,
        out_weight.T, lengths,
    )
    return jnp.transpose(blocks, (1, 0, 2)).reshape(rows, 2 * PLANE * columns)


def solution(mesh):
    fused = mesh.shape["mp"] == 2 and mesh.shape["blk"] == PLANE * PLANE
    placed = (
        P("blk", "mp"),
        P("blk", "mp"),
        P("blk", "mp"),
        P("blk", "mp"),
        P("blk", "mp"),
        P("mp", "blk"),
        P(),
    )
    return jax.shard_map(
        per_device_fused if fused else per_device, mesh=mesh, in_specs=placed, out_specs=P("blk", "mp"), check_vma=False
    )
```

```python
import math

import jax
import jax.numpy as jnp
from jax import lax
from jax.experimental import pallas as pl
from jax.experimental.pallas import tpu as pltpu
from jax.sharding import PartitionSpec as P

HEAD_SIZE = 128


MASKED_SCORE = -1e30


def passed_along(block, axis, distance):
    devices = range(lax.axis_size(axis))
    route = [(i - distance, i) for i in devices if i - distance in devices]
    return lax.ppermute(block, axis, route)


def per_device(
    queries,
    suffix_key_rows,
    suffix_value_rows,
    shared_prefix_keys,
    shared_prefix_values,
    out_weight,
    lengths,
):
    tok_rows = queries.shape[0]
    kv_heads = suffix_key_rows.shape[1] // HEAD_SIZE
    q_heads = queries.shape[1] // HEAD_SIZE
    heads_per_group = q_heads // kv_heads
    blocks = lax.axis_size("blk")
    cycle_reach = blocks // 4
    my_block = lax.axis_index("blk")
    score_scale = 1.0 / math.sqrt(HEAD_SIZE)
    heads_of_query = queries.reshape(tok_rows, kv_heads, heads_per_group, HEAD_SIZE)
    req_ends = jnp.cumsum(lengths)
    local_rows = jnp.arange(tok_rows, dtype=jnp.int32)
    query_pos = my_block * tok_rows + local_rows

    def owner_of(position):
        return jnp.sum((position[:, None] >= req_ends[None, :]).astype(jnp.int32), axis=1)

    query_owner = owner_of(query_pos)

    def update(carry_state, key_block, value_block, visible):
        run_max, row_total, accumulated = carry_state
        count = key_block.shape[0]
        key_heads = key_block.reshape(count, kv_heads, HEAD_SIZE)
        value_heads = value_block.reshape(count, kv_heads, HEAD_SIZE)
        scores = (
            jnp.einsum(
                "qhgd,khd->hgqk", heads_of_query, key_heads, preferred_element_type=jnp.float32
            )
            * score_scale
        )
        if visible is not None:
            scores = jnp.where(visible[None, None], scores, MASKED_SCORE)
        new_max = jnp.maximum(run_max, jnp.max(scores, axis=-1))
        weights = jnp.exp(scores - new_max[..., None])
        if visible is not None:
            weights = jnp.where(visible[None, None], weights, 0.0)
        rescale = jnp.exp(run_max - new_max)
        row_total = row_total * rescale + jnp.sum(weights, axis=-1)
        contrib = jnp.einsum(
            "hgqk,khd->hgqd",
            weights.astype(jnp.bfloat16),
            value_heads,
            preferred_element_type=jnp.float32,
        )
        accumulated = accumulated * rescale[..., None] + contrib
        return (new_max, row_total, accumulated)

    start_state = (
        jnp.full((kv_heads, heads_per_group, tok_rows), MASKED_SCORE, jnp.float32),
        jnp.zeros((kv_heads, heads_per_group, tok_rows), jnp.float32),
        jnp.zeros((kv_heads, heads_per_group, tok_rows, HEAD_SIZE), jnp.float32),
    )
    carry_state = update(
        start_state,
        lax.all_gather(shared_prefix_keys, "blk", axis=0, tiled=True),
        lax.all_gather(shared_prefix_values, "blk", axis=0, tiled=True),
        None,
    )

    def visible_from(distance):
        key_pos = (my_block - distance) * tok_rows + local_rows
        key_owner = owner_of(key_pos)
        return (
            (key_owner[None, :] == query_owner[:, None])
            & (key_pos[None, :] <= query_pos[:, None])
            & (key_pos[None, :] >= 0)
        )

    kv_pair = jnp.stack((suffix_key_rows, suffix_value_rows))
    carry_state = update(carry_state, kv_pair[0], kv_pair[1], visible_from(0))

    def advance(distance, loop_carry):
        current, moving = loop_carry
        moving = passed_along(moving, "blk", 1)
        visible = visible_from(distance)
        current = update(current, moving[0], moving[1], visible)
        return (current, moving)

    carry_state, kv_pair = lax.fori_loop(1, cycle_reach + 1, advance, (carry_state, kv_pair))
    run_max, row_total, accumulated = carry_state
    attended = accumulated / row_total[..., None]
    attn = (
        jnp.transpose(attended, (2, 0, 1, 3))
        .reshape(tok_rows, q_heads * HEAD_SIZE)
        .astype(jnp.bfloat16)
    )
    product = jnp.dot(
        attn,
        lax.all_gather(out_weight, "blk", axis=1, tiled=True),
        preferred_element_type=jnp.float32,
    )
    return lax.psum_scatter(product.astype(jnp.bfloat16), "mp", scatter_dimension=1, tiled=True)


MESH = pl.DeviceIdType.MESH
NT = (((1,), (1,)), ((), ()))
REACH = 4
PLANE = 4
PIECES = 4


def fused_kernel(
    q_ref, k_ref, v_ref, pk_ref, pv_ref, w_ref, len_ref,
    out_ref,
    queries, keys, values, bias, weights, attn, mine, to_core, from_core, summed,
    local, pz_s, pz_r, pp_s, pp_r, sx_s, sx_r, w_s, w_r, at_s, at_r, mp_s, mp_r, out_s, out_r,
):
    rows = q_ref.shape[0]
    kv_heads = k_ref.shape[1] // HEAD_SIZE
    group = q_ref.shape[1] // k_ref.shape[1]
    part = pk_ref.shape[0]
    prefix = part * PLANE * PLANE
    chunk = part * PLANE
    me = lax.axis_index("blk")
    mp = lax.axis_index("mp")
    z = lax.div(me, PLANE)
    i = lax.rem(me, PLANE)
    z_hi, z_lo = lax.div(z, 2), lax.rem(z, 2)
    y, x = lax.div(i, 2), lax.rem(i, 2)
    x_mate = me + 1 - 2 * x
    y_mate = me + 2 * (1 - 2 * y)
    near = me + PLANE * (1 - 2 * z_lo)
    far = me + 2 * PLANE * (1 - 2 * z_hi)
    across = near + 1 - 2 * x
    shard = z_hi * 2 + y
    far_shard = (1 - z_hi) * 2 + y
    token = z_lo * 2 + x
    near_token = (1 - z_lo) * 2 + x
    x_token = z_lo * 2 + 1 - x

    def send(src, dst, send_sem, recv_sem, blk, core=None):
        return pltpu.make_async_remote_copy(
            src_ref=src, dst_ref=dst, send_sem=send_sem, recv_sem=recv_sem,
            device_id=(blk, mp if core is None else core), device_id_type=MESH,
        )

    def in_column(o):
        return lax.rem(z + o, PLANE) * PLANE + i

    def in_plane(o):
        return z * PLANE + lax.rem(i + o, PLANE)

    barrier = pltpu.get_barrier_semaphore()
    for o in (1, 2, 3):
        pl.semaphore_signal(barrier, inc=1, device_id=(in_column(o), mp), device_id_type=MESH)
        pl.semaphore_signal(barrier, inc=1, device_id=(in_plane(o), mp), device_id_type=MESH)
    pl.semaphore_signal(barrier, inc=1, device_id=(across, mp), device_id_type=MESH)
    pl.semaphore_signal(barrier, inc=1, device_id=(me, 1 - mp), device_id_type=MESH)

    own_rows = pl.ds(pl.multiple_of(i * chunk + z * part, part), part)
    own_copies = [
        pltpu.make_async_copy(source, target, local.at[n])
        for n, (source, target) in enumerate((
            (pk_ref, keys.at[own_rows]),
            (pv_ref, values.at[own_rows]),
            (k_ref, keys.at[pl.ds(prefix, rows)]),
            (v_ref, values.at[pl.ds(prefix, rows)]),
            (q_ref, queries),
            (w_ref, weights.at[shard]),
        ))
    ]
    for copy in own_copies:
        copy.start()
    pl.semaphore_wait(barrier, 8)

    kv = ((k_ref, pk_ref, keys), (v_ref, pv_ref, values))

    def suffix_rows(d):
        return pl.ds(prefix + d * rows, rows)

    def up_copy(c):
        own, _, held = kv[c]
        return send(own, held.at[suffix_rows(REACH)], sx_s.at[REACH, c], sx_r.at[REACH, c],
                    me + REACH)

    def prefix_up(o, c):
        _, own, held = kv[c]
        return send(own, held.at[own_rows], pz_s.at[o, c], pz_r.at[o, c], in_column(o))

    my_chunk = pl.ds(pl.multiple_of(i * chunk, chunk), chunk)

    def prefix_across(o, c):
        held = kv[c][2]
        return send(held.at[my_chunk], held.at[my_chunk], pp_s.at[o, c], pp_r.at[o, c],
                    in_plane(o))

    def across_own(d, c):
        own, _, held = kv[c]
        return send(own, held.at[suffix_rows(d)], sx_s.at[d, c], sx_r.at[d, c], in_plane(d))

    def across_relayed(d, c):
        held = kv[c][2]
        return send(held.at[suffix_rows(REACH)], held.at[suffix_rows(d)], sx_s.at[d, c],
                    sx_r.at[d, c], in_plane(d))

    piece = w_ref.shape[0] // PIECES

    def to_far(c):
        at = pl.ds(c * piece, piece)
        return send(w_ref.at[at], weights.at[shard, at], w_s.at[0, c], w_r.at[0, c], far)

    def to_y(c):
        at = pl.ds(c * piece, piece)
        return send(w_ref.at[at], weights.at[shard, at], w_s.at[1, c], w_r.at[1, c], y_mate)

    def far_to_y(c):
        block = weights.at[far_shard, pl.ds(c * piece, piece)]
        return send(block, block, w_s.at[2, c], w_r.at[2, c], y_mate)

    def pass_on(c):
        to_far(c).wait_recv()
        far_to_y(c).start()

    for o in (1, 2, 3):
        for c in (0, 1):
            prefix_up(o, c).start()

    @pl.when(z + 1 < PLANE)
    def _():
        up_copy(0).start()
        up_copy(1).start()

    for d in (1, 2, 3):
        @pl.when(i + d < PLANE)
        def _():
            across_own(d, 0).start()
            across_own(d, 1).start()

    for d in range(1, REACH + 1):
        @pl.when(me < d)
        def _():
            keys[suffix_rows(d), :] = jnp.zeros((rows, keys.shape[1]), keys.dtype)
            values[suffix_rows(d), :] = jnp.zeros((rows, keys.shape[1]), keys.dtype)

    query_pos = me * rows + lax.broadcasted_iota(jnp.int32, (rows, HEAD_SIZE), 0)
    first = jnp.zeros((rows, HEAD_SIZE), jnp.int32)
    end = jnp.int32(0)
    for r in range(len_ref.shape[0]):
        end = end + len_ref[r]
        first = jnp.maximum(first, jnp.where(query_pos >= end, end, 0))
    lane = lax.broadcasted_iota(jnp.int32, (rows, HEAD_SIZE), 1)
    for d in range(REACH + 1):
        for t in range(rows // HEAD_SIZE):
            key_pos = (me - d) * rows + t * HEAD_SIZE + lane
            seen = (key_pos >= first) & (key_pos <= query_pos)
            at = d * rows + t * HEAD_SIZE
            bias[:, at:at + HEAD_SIZE] = jnp.where(seen, 0.0, MASKED_SCORE)

    for copy in own_copies:
        copy.wait()
    for o in (1, 2, 3):
        for c in (0, 1):
            prefix_up(o, c).wait_recv()
    for o in (1, 2, 3):
        for c in (0, 1):
            prefix_across(o, c).start()

    @pl.when(z >= 1)
    def _():
        up_copy(0).wait_recv()
        up_copy(1).wait_recv()
        for d in (1, 2, 3):
            @pl.when(i + d >= PLANE)
            def _():
                across_relayed(d, 0).start()
                across_relayed(d, 1).start()

    for c in range(PIECES):
        to_far(c).start()
    to_y(0).start()

    for o in (1, 2, 3):
        for c in (0, 1):
            prefix_across(o, c).wait_recv()
    for d in (1, 2, 3):
        @pl.when(me >= d)
        def _():
            across_own(d, 0).wait_recv()
            across_own(d, 1).wait_recv()
    for c in range(1, PIECES):
        to_y(c).start()

    exponent_scale = math.log2(math.e) / math.sqrt(HEAD_SIZE)
    width = group * HEAD_SIZE

    def attn_block(t, g):
        columns = pl.ds(pl.multiple_of(g * width, HEAD_SIZE), width)
        return attn.at[t, :, columns]

    def attn_to_x(g):
        block = attn_block(token, g)
        return send(block, block, at_s.at[g, 0], at_r.at[g, 0], x_mate)

    def attn_to_near(g):
        block = attn_block(token, g)
        return send(block, block, at_s.at[g, 1], at_r.at[g, 1], near)

    def near_to_x(g):
        block = attn_block(near_token, g)
        return send(block, block, at_s.at[g, 2], at_r.at[g, 2], x_mate)

    def x_to_near(g):
        block = attn_block(x_token, g)
        return send(block, block, at_s.at[g, 2], at_r.at[g, 2], near)

    def attn_pass_on(g):
        attn_to_x(g).wait_recv()
        attn_to_near(g).wait_recv()

        @pl.when(lax.rem(g, 2) == 0)
        def _():
            near_to_x(g).start()

        @pl.when(lax.rem(g, 2) == 1)
        def _():
            x_to_near(g).start()

    def one_group(g, carry):
        head = pl.ds(pl.multiple_of(g * HEAD_SIZE, HEAD_SIZE), HEAD_SIZE)
        for h in range(group):
            column = pl.ds(pl.multiple_of(g * width + h * HEAD_SIZE, HEAD_SIZE), HEAD_SIZE)
            q = queries[:, column]
            s_pre = lax.dot_general(q, keys[:prefix, head], NT, preferred_element_type=jnp.float32)
            s_suf = lax.dot_general(q, keys[prefix:, head], NT, preferred_element_type=jnp.float32)
            s_suf = s_suf + bias[...]
            peak = jnp.maximum(
                jnp.max(s_pre, axis=1, keepdims=True), jnp.max(s_suf, axis=1, keepdims=True)
            )
            p_pre = jnp.exp2((s_pre - peak) * exponent_scale)
            p_suf = jnp.exp2((s_suf - peak) * exponent_scale)
            total = jnp.sum(p_pre, axis=1, keepdims=True) + jnp.sum(p_suf, axis=1, keepdims=True)
            mixed = jnp.dot(
                p_pre.astype(jnp.bfloat16), values[:prefix, head],
                preferred_element_type=jnp.float32,
            ) + jnp.dot(
                p_suf.astype(jnp.bfloat16), values[prefix:, head],
                preferred_element_type=jnp.float32,
            )
            attn[token, :, column] = (mixed / total).astype(jnp.bfloat16)
        attn_to_x(g).start()
        attn_to_near(g).start()

        @pl.when(g >= 1)
        def _():
            attn_pass_on(g - 1)

        return carry

    lax.fori_loop(0, kv_heads, one_group, 0)
    attn_pass_on(jnp.int32(kv_heads - 1))
    for c in range(PIECES):
        pass_on(c)

    def take_across(g, carry):
        near_to_x(g).wait_recv()
        return carry

    lax.fori_loop(0, kv_heads, take_across, 0)

    def to_sibling(low, t):
        return send(to_core.at[low, t], from_core.at[low, t], mp_s.at[low, t], mp_r.at[low, t],
                    me, 1 - mp)

    def member(t):
        return (z_hi * 2 + lax.div(t, 2)) * PLANE + y * 2 + lax.rem(t, 2)

    def column_block(t, low):
        return lax.div(t, 2) * PLANE + low * 2 + lax.rem(t, 2)

    def to_owner(low, t):
        return send(summed.at[low, t], out_ref.at[column_block(token, low)], out_s.at[low, t],
                    out_r.at[low, token], member(t))

    def out_arrival(low, t):
        return send(summed.at[low, t], out_ref.at[column_block(t, low)], out_s.at[low, t],
                    out_r.at[low, t], member(t))

    def one_shard(n, carry):
        hi = z_hi + lax.div(n, 2) * (1 - 2 * z_hi)
        low = y + lax.rem(n, 2) * (1 - 2 * y)
        src = hi * 2 + low
        ours = hi == mp

        @pl.when(n == 1)
        def _():
            for c in range(PIECES):
                to_y(c).wait_recv()

        @pl.when(n == 3)
        def _():
            for c in range(PIECES):
                far_to_y(c).wait_recv()

        def one_block(t, c):
            product = lax.dot_general(
                attn[t], weights[src], NT, preferred_element_type=jnp.float32
            ).astype(jnp.bfloat16)

            @pl.when(ours)
            def _():
                mine[t] = product

            @pl.when(jnp.logical_not(ours))
            def _():
                to_core[low, t] = product
                to_sibling(low, t).start()

            return c

        lax.fori_loop(0, PLANE, one_block, 0)

        @pl.when(ours)
        def _():
            def add_block(t, c):
                to_sibling(low, t).wait_recv()
                both = mine[t].astype(jnp.float32) + from_core[low, t].astype(jnp.float32)
                both = both.astype(jnp.bfloat16)

                @pl.when(t == token)
                def _():
                    out_ref[column_block(token, low)] = both

                @pl.when(t != token)
                def _():
                    summed[low, t] = both
                    to_owner(low, t).start()

                return c

            lax.fori_loop(0, PLANE, add_block, 0)

        return carry

    lax.fori_loop(0, PLANE, one_shard, 0)

    for low in (0, 1):
        for t in range(PLANE):
            to_sibling(low, t).wait_send()

            @pl.when(t != token)
            def _():
                out_arrival(low, t).wait_recv()
                out_arrival(low, t).wait_send()

    for o in (1, 2, 3):
        for c in (0, 1):
            prefix_up(o, c).wait_send()
            prefix_across(o, c).wait_send()
            across_own_sent = across_own(o, c)

            @pl.when((i + o < PLANE) | (z >= 1))
            def _():
                across_own_sent.wait_send()
    for c in (0, 1):
        @pl.when(z + 1 < PLANE)
        def _():
            up_copy(c).wait_send()
    for c in range(PIECES):
        to_far(c).wait_send()
        to_y(c).wait_send()
        far_to_y(c).wait_send()
    for g in range(kv_heads):
        attn_to_x(g).wait_send()
        attn_to_near(g).wait_send()
        near_to_x(g).wait_send()


def per_device_fused(
    queries,
    suffix_key_rows,
    suffix_value_rows,
    shared_prefix_keys,
    shared_prefix_values,
    out_weight,
    lengths,
):
    rows, q_cols = queries.shape
    kv_cols = suffix_key_rows.shape[1]
    columns = out_weight.shape[1]
    held = shared_prefix_keys.shape[0] * PLANE * PLANE + (REACH + 1) * rows
    kv_heads = kv_cols // HEAD_SIZE
    vmem = pl.BlockSpec(memory_space=pltpu.VMEM)
    low = jnp.bfloat16
    sem = pltpu.SemaphoreType.DMA
    blocks = pl.pallas_call(
        fused_kernel,
        out_shape=jax.ShapeDtypeStruct((2 * PLANE, rows, columns), low),
        in_specs=[pl.BlockSpec(memory_space=pl.ANY)] * 6 + [pl.BlockSpec(memory_space=pltpu.SMEM)],
        out_specs=vmem,
        scratch_shapes=[
            pltpu.VMEM((rows, q_cols), low),
            pltpu.VMEM((held, kv_cols), low),
            pltpu.VMEM((held, kv_cols), low),
            pltpu.VMEM((rows, (REACH + 1) * rows), jnp.float32),
            pltpu.VMEM((PLANE, columns, q_cols), low),
            pltpu.VMEM((PLANE, rows, q_cols), low),
            pltpu.VMEM((PLANE, rows, columns), low),
            pltpu.VMEM((2, PLANE, rows, columns), low),
            pltpu.VMEM((2, PLANE, rows, columns), low),
            pltpu.VMEM((2, PLANE, rows, columns), low),
            sem((6,)), sem((4, 2)), sem((4, 2)), sem((4, 2)), sem((4, 2)),
            sem((REACH + 1, 2)), sem((REACH + 1, 2)),
            sem((3, PIECES)), sem((3, PIECES)),
            sem((kv_heads, 3)), sem((kv_heads, 3)),
            sem((2, PLANE)), sem((2, PLANE)), sem((2, PLANE)), sem((2, PLANE)),
        ],
        compiler_params=pltpu.CompilerParams(
            collective_id=0, has_side_effects=True, vmem_limit_bytes=60 * 1024 * 1024
        ),
        cost_estimate=pl.CostEstimate(
            flops=12_000_000_000, bytes_accessed=8_000_000, transcendentals=10_000_000
        ),
    )(
        queries, suffix_key_rows, suffix_value_rows, shared_prefix_keys, shared_prefix_values,
        out_weight.T, lengths,
    )
    return jnp.transpose(blocks, (1, 0, 2)).reshape(rows, 2 * PLANE * columns)


def solution(mesh):
    fused = mesh.shape["mp"] == 2 and mesh.shape["blk"] == PLANE * PLANE
    placed = (
        P("blk", "mp"),
        P("blk", "mp"),
        P("blk", "mp"),
        P("blk", "mp"),
        P("blk", "mp"),
        P("mp", "blk"),
        P(),
    )
    return jax.shard_map(
        per_device_fused if fused else per_device, mesh=mesh, in_specs=placed, out_specs=P("blk", "mp"), check_vma=False
    )
```

```python
import math

import jax
import jax.numpy as jnp
from jax import lax
from jax.experimental import pallas as pl
from jax.experimental.pallas import tpu as pltpu
from jax.sharding import PartitionSpec as P

HEAD_SIZE = 128


MASKED_SCORE = -1e30


def passed_along(block, axis, distance):
    devices = range(lax.axis_size(axis))
    route = [(i - distance, i) for i in devices if i - distance in devices]
    return lax.ppermute(block, axis, route)


def per_device(
    queries,
    suffix_key_rows,
    suffix_value_rows,
    shared_prefix_keys,
    shared_prefix_values,
    out_weight,
    lengths,
):
    tok_rows = queries.shape[0]
    kv_heads = suffix_key_rows.shape[1] // HEAD_SIZE
    q_heads = queries.shape[1] // HEAD_SIZE
    heads_per_group = q_heads // kv_heads
    blocks = lax.axis_size("blk")
    cycle_reach = blocks // 4
    my_block = lax.axis_index("blk")
    score_scale = 1.0 / math.sqrt(HEAD_SIZE)
    heads_of_query = queries.reshape(tok_rows, kv_heads, heads_per_group, HEAD_SIZE)
    req_ends = jnp.cumsum(lengths)
    local_rows = jnp.arange(tok_rows, dtype=jnp.int32)
    query_pos = my_block * tok_rows + local_rows

    def owner_of(position):
        return jnp.sum((position[:, None] >= req_ends[None, :]).astype(jnp.int32), axis=1)

    query_owner = owner_of(query_pos)

    def update(carry_state, key_block, value_block, visible):
        run_max, row_total, accumulated = carry_state
        count = key_block.shape[0]
        key_heads = key_block.reshape(count, kv_heads, HEAD_SIZE)
        value_heads = value_block.reshape(count, kv_heads, HEAD_SIZE)
        scores = (
            jnp.einsum(
                "qhgd,khd->hgqk", heads_of_query, key_heads, preferred_element_type=jnp.float32
            )
            * score_scale
        )
        if visible is not None:
            scores = jnp.where(visible[None, None], scores, MASKED_SCORE)
        new_max = jnp.maximum(run_max, jnp.max(scores, axis=-1))
        weights = jnp.exp(scores - new_max[..., None])
        if visible is not None:
            weights = jnp.where(visible[None, None], weights, 0.0)
        rescale = jnp.exp(run_max - new_max)
        row_total = row_total * rescale + jnp.sum(weights, axis=-1)
        contrib = jnp.einsum(
            "hgqk,khd->hgqd",
            weights.astype(jnp.bfloat16),
            value_heads,
            preferred_element_type=jnp.float32,
        )
        accumulated = accumulated * rescale[..., None] + contrib
        return (new_max, row_total, accumulated)

    start_state = (
        jnp.full((kv_heads, heads_per_group, tok_rows), MASKED_SCORE, jnp.float32),
        jnp.zeros((kv_heads, heads_per_group, tok_rows), jnp.float32),
        jnp.zeros((kv_heads, heads_per_group, tok_rows, HEAD_SIZE), jnp.float32),
    )
    carry_state = update(
        start_state,
        lax.all_gather(shared_prefix_keys, "blk", axis=0, tiled=True),
        lax.all_gather(shared_prefix_values, "blk", axis=0, tiled=True),
        None,
    )

    def visible_from(distance):
        key_pos = (my_block - distance) * tok_rows + local_rows
        key_owner = owner_of(key_pos)
        return (
            (key_owner[None, :] == query_owner[:, None])
            & (key_pos[None, :] <= query_pos[:, None])
            & (key_pos[None, :] >= 0)
        )

    kv_pair = jnp.stack((suffix_key_rows, suffix_value_rows))
    carry_state = update(carry_state, kv_pair[0], kv_pair[1], visible_from(0))

    def advance(distance, loop_carry):
        current, moving = loop_carry
        moving = passed_along(moving, "blk", 1)
        visible = visible_from(distance)
        current = update(current, moving[0], moving[1], visible)
        return (current, moving)

    carry_state, kv_pair = lax.fori_loop(1, cycle_reach + 1, advance, (carry_state, kv_pair))
    run_max, row_total, accumulated = carry_state
    attended = accumulated / row_total[..., None]
    attn = (
        jnp.transpose(attended, (2, 0, 1, 3))
        .reshape(tok_rows, q_heads * HEAD_SIZE)
        .astype(jnp.bfloat16)
    )
    product = jnp.dot(
        attn,
        lax.all_gather(out_weight, "blk", axis=1, tiled=True),
        preferred_element_type=jnp.float32,
    )
    return lax.psum_scatter(product.astype(jnp.bfloat16), "mp", scatter_dimension=1, tiled=True)


MESH = pl.DeviceIdType.MESH
NT = (((1,), (1,)), ((), ()))
REACH = 4
PLANE = 4


def fused_kernel(
    q_ref, k_ref, v_ref, pk_ref, pv_ref, w_ref, len_ref,
    out_ref,
    queries, keys, values, bias, weights, attn, mine, to_core, from_core, summed,
    local, pz_s, pz_r, pp_s, pp_r, sx_s, sx_r, w_s, w_r, at_s, at_r, mp_s, mp_r, out_s, out_r,
):
    rows = q_ref.shape[0]
    kv_heads = k_ref.shape[1] // HEAD_SIZE
    group = q_ref.shape[1] // k_ref.shape[1]
    part = pk_ref.shape[0]
    prefix = part * PLANE * PLANE
    chunk = part * PLANE
    me = lax.axis_index("blk")
    mp = lax.axis_index("mp")
    z = lax.div(me, PLANE)
    i = lax.rem(me, PLANE)

    def send(src, dst, send_sem, recv_sem, blk, core=None):
        return pltpu.make_async_remote_copy(
            src_ref=src, dst_ref=dst, send_sem=send_sem, recv_sem=recv_sem,
            device_id=(blk, mp if core is None else core), device_id_type=MESH,
        )

    def in_column(o):
        return lax.rem(z + o, PLANE) * PLANE + i

    def in_plane(o):
        return z * PLANE + lax.rem(i + o, PLANE)

    barrier = pltpu.get_barrier_semaphore()
    for o in (1, 2, 3):
        pl.semaphore_signal(barrier, inc=1, device_id=(in_column(o), mp), device_id_type=MESH)
        pl.semaphore_signal(barrier, inc=1, device_id=(in_plane(o), mp), device_id_type=MESH)
    pl.semaphore_signal(barrier, inc=1, device_id=(me, 1 - mp), device_id_type=MESH)

    own_rows = pl.ds(pl.multiple_of(i * chunk + z * part, part), part)
    own_copies = [
        pltpu.make_async_copy(source, target, local.at[n])
        for n, (source, target) in enumerate((
            (pk_ref, keys.at[own_rows]),
            (pv_ref, values.at[own_rows]),
            (k_ref, keys.at[pl.ds(prefix, rows)]),
            (v_ref, values.at[pl.ds(prefix, rows)]),
            (q_ref, queries),
            (w_ref, weights.at[z]),
        ))
    ]
    for copy in own_copies:
        copy.start()
    pl.semaphore_wait(barrier, 7)

    kv = ((k_ref, pk_ref, keys), (v_ref, pv_ref, values))

    def suffix_rows(d):
        return pl.ds(prefix + d * rows, rows)

    def up_copy(c):
        own, _, held = kv[c]
        return send(own, held.at[suffix_rows(REACH)], sx_s.at[REACH, c], sx_r.at[REACH, c],
                    me + REACH)

    def prefix_up(o, c):
        _, own, held = kv[c]
        return send(own, held.at[own_rows], pz_s.at[o, c], pz_r.at[o, c], in_column(o))

    my_chunk = pl.ds(pl.multiple_of(i * chunk, chunk), chunk)

    def prefix_across(o, c):
        held = kv[c][2]
        return send(held.at[my_chunk], held.at[my_chunk], pp_s.at[o, c], pp_r.at[o, c],
                    in_plane(o))

    def across_own(d, c):
        own, _, held = kv[c]
        return send(own, held.at[suffix_rows(d)], sx_s.at[d, c], sx_r.at[d, c], in_plane(d))

    def across_relayed(d, c):
        held = kv[c][2]
        return send(held.at[suffix_rows(REACH)], held.at[suffix_rows(d)], sx_s.at[d, c],
                    sx_r.at[d, c], in_plane(d))

    def weight_hop(way, k):
        origin = z - (k - 1) if way == 0 else z + (k - 1)
        to = me + PLANE if way == 0 else me - PLANE
        source = w_ref if k == 1 else weights.at[origin]
        return send(source, weights.at[origin], w_s.at[way, k], w_r.at[way, k], to)

    def sends_hop(way, k):
        if way == 0:
            return (z - (k - 1) >= 0) & (z + 1 < PLANE)
        return (z + (k - 1) < PLANE) & (z >= 1)

    def gets_hop(way, k):
        return z - k >= 0 if way == 0 else z + k < PLANE

    def start_hop(k):
        for way in (0, 1):
            @pl.when(sends_hop(way, k))
            def _():
                weight_hop(way, k).start()

    def take_hop(k):
        for way in (0, 1):
            @pl.when(gets_hop(way, k))
            def _():
                weight_hop(way, k).wait_recv()

    for o in (1, 2, 3):
        for c in (0, 1):
            prefix_up(o, c).start()

    @pl.when(z + 1 < PLANE)
    def _():
        up_copy(0).start()
        up_copy(1).start()

    for d in (1, 2, 3):
        @pl.when(i + d < PLANE)
        def _():
            across_own(d, 0).start()
            across_own(d, 1).start()

    for d in range(1, REACH + 1):
        @pl.when(me < d)
        def _():
            keys[suffix_rows(d), :] = jnp.zeros((rows, keys.shape[1]), keys.dtype)
            values[suffix_rows(d), :] = jnp.zeros((rows, keys.shape[1]), keys.dtype)

    query_pos = me * rows + lax.broadcasted_iota(jnp.int32, (rows, HEAD_SIZE), 0)
    first = jnp.zeros((rows, HEAD_SIZE), jnp.int32)
    end = jnp.int32(0)
    for r in range(len_ref.shape[0]):
        end = end + len_ref[r]
        first = jnp.maximum(first, jnp.where(query_pos >= end, end, 0))
    lane = lax.broadcasted_iota(jnp.int32, (rows, HEAD_SIZE), 1)
    for d in range(REACH + 1):
        for t in range(rows // HEAD_SIZE):
            key_pos = (me - d) * rows + t * HEAD_SIZE + lane
            seen = (key_pos >= first) & (key_pos <= query_pos)
            at = d * rows + t * HEAD_SIZE
            bias[:, at:at + HEAD_SIZE] = jnp.where(seen, 0.0, MASKED_SCORE)

    for copy in own_copies:
        copy.wait()
    for o in (1, 2, 3):
        for c in (0, 1):
            prefix_up(o, c).wait_recv()
    for o in (1, 2, 3):
        for c in (0, 1):
            prefix_across(o, c).start()

    @pl.when(z >= 1)
    def _():
        up_copy(0).wait_recv()
        up_copy(1).wait_recv()
        for d in (1, 2, 3):
            @pl.when(i + d >= PLANE)
            def _():
                across_relayed(d, 0).start()
                across_relayed(d, 1).start()

    @pl.when(z + 1 < PLANE)
    def _():
        up_copy(0).wait_send()
        up_copy(1).wait_send()

    start_hop(1)

    for o in (1, 2, 3):
        for c in (0, 1):
            prefix_across(o, c).wait_recv()
    for d in (1, 2, 3):
        @pl.when(me >= d)
        def _():
            across_own(d, 0).wait_recv()
            across_own(d, 1).wait_recv()

    exponent_scale = math.log2(math.e) / math.sqrt(HEAD_SIZE)
    width = group * HEAD_SIZE

    def attn_part(g, o):
        columns = pl.ds(pl.multiple_of(g * width, HEAD_SIZE), width)
        block = attn.at[i, :, columns]
        return send(block, block, at_s.at[g, o], at_r.at[g, o], in_plane(o))

    def one_group(g, carry):
        head = pl.ds(pl.multiple_of(g * HEAD_SIZE, HEAD_SIZE), HEAD_SIZE)
        for h in range(group):
            column = pl.ds(pl.multiple_of(g * width + h * HEAD_SIZE, HEAD_SIZE), HEAD_SIZE)
            q = queries[:, column]
            s_pre = lax.dot_general(q, keys[:prefix, head], NT, preferred_element_type=jnp.float32)
            s_suf = lax.dot_general(q, keys[prefix:, head], NT, preferred_element_type=jnp.float32)
            s_suf = s_suf + bias[...]
            peak = jnp.maximum(
                jnp.max(s_pre, axis=1, keepdims=True), jnp.max(s_suf, axis=1, keepdims=True)
            )
            p_pre = jnp.exp2((s_pre - peak) * exponent_scale)
            p_suf = jnp.exp2((s_suf - peak) * exponent_scale)
            total = jnp.sum(p_pre, axis=1, keepdims=True) + jnp.sum(p_suf, axis=1, keepdims=True)
            mixed = jnp.dot(
                p_pre.astype(jnp.bfloat16), values[:prefix, head],
                preferred_element_type=jnp.float32,
            ) + jnp.dot(
                p_suf.astype(jnp.bfloat16), values[prefix:, head],
                preferred_element_type=jnp.float32,
            )
            attn[i, :, column] = (mixed / total).astype(jnp.bfloat16)
        for o in (1, 2, 3):
            attn_part(g, o).start()

        @pl.when(g == 1)
        def _():
            take_hop(1)
            start_hop(2)

        return carry

    lax.fori_loop(0, kv_heads, one_group, 0)

    take_hop(2)
    start_hop(3)

    def to_sibling(low, t):
        return send(to_core.at[low, t], from_core.at[low, t], mp_s.at[low, t], mp_r.at[low, t],
                    me, 1 - mp)

    def to_owner(low, t):
        return send(summed.at[low, t], out_ref.at[low * PLANE + i], out_s.at[low, t],
                    out_r.at[low, i], z * PLANE + t)

    def out_arrival(low, t):
        return send(summed.at[low, t], out_ref.at[low * PLANE + t], out_s.at[low, t],
                    out_r.at[low, t], z * PLANE + t)

    def shard(n):
        inner = lax.div(z * (3 - z), 2)
        f = n + inner * (1 - 2 * n) * (1 - lax.div(n, 2))
        src = f + lax.div(z, 2) * (3 - 2 * f)
        return src, lax.rem(src, 2), lax.div(src, 2) == mp

    def rows_from(o):
        return lax.rem(i - o + PLANE, PLANE)

    def multiply(n, t):
        src, low, ours = shard(n)
        product = lax.dot_general(
            attn[t], weights[src], NT, preferred_element_type=jnp.float32
        ).astype(jnp.bfloat16)

        @pl.when(ours)
        def _():
            mine[low, t] = product

        @pl.when(jnp.logical_not(ours))
        def _():
            to_core[low, t] = product
            to_sibling(low, t).start()

    def add(n, t):
        src, low, ours = shard(n)

        @pl.when(ours)
        def _():
            to_sibling(low, t).wait_recv()
            both = mine[low, t].astype(jnp.float32) + from_core[low, t].astype(jnp.float32)
            both = both.astype(jnp.bfloat16)

            @pl.when(t == i)
            def _():
                out_ref[low * PLANE + i] = both

            @pl.when(t != i)
            def _():
                summed[low, t] = both
                to_owner(low, t).start()

    def one_source(o, carry):
        for v in (1, 2, 3):
            @pl.when(o == v)
            def _():
                for g in range(kv_heads):
                    attn_part(g, v).wait_recv()

        def times(n, c):
            multiply(n, rows_from(o))
            return c

        lax.fori_loop(0, PLANE - 1, times, 0)

        @pl.when(o >= 1)
        def _():
            def plus(n, c):
                add(n, rows_from(o - 1))
                return c

            lax.fori_loop(0, PLANE - 1, plus, 0)

        return carry

    lax.fori_loop(0, PLANE, one_source, 0)
    for n in range(PLANE - 1):
        add(jnp.int32(n), rows_from(PLANE - 1))

    take_hop(3)

    def last_shard(o, carry):
        multiply(jnp.int32(PLANE - 1), rows_from(PLANE - 1 - o))

        @pl.when(o >= 1)
        def _():
            add(jnp.int32(PLANE - 1), rows_from(PLANE - o))

        return carry

    lax.fori_loop(0, PLANE, last_shard, 0)
    add(jnp.int32(PLANE - 1), rows_from(0))

    for low in (0, 1):
        for t in range(PLANE):
            to_sibling(low, t).wait_send()

            @pl.when(t != i)
            def _():
                out_arrival(low, t).wait_recv()
                out_arrival(low, t).wait_send()

    for o in (1, 2, 3):
        for c in (0, 1):
            prefix_up(o, c).wait_send()
            prefix_across(o, c).wait_send()
            across_own_sent = across_own(o, c)

            @pl.when((i + o < PLANE) | (z >= 1))
            def _():
                across_own_sent.wait_send()
        for g in range(kv_heads):
            attn_part(g, o).wait_send()
    for k in (1, 2, 3):
        for way in (0, 1):
            @pl.when(sends_hop(way, k))
            def _():
                weight_hop(way, k).wait_send()


def per_device_fused(
    queries,
    suffix_key_rows,
    suffix_value_rows,
    shared_prefix_keys,
    shared_prefix_values,
    out_weight,
    lengths,
):
    rows, q_cols = queries.shape
    kv_cols = suffix_key_rows.shape[1]
    columns = out_weight.shape[1]
    held = shared_prefix_keys.shape[0] * PLANE * PLANE + (REACH + 1) * rows
    kv_heads = kv_cols // HEAD_SIZE
    vmem = pl.BlockSpec(memory_space=pltpu.VMEM)
    low = jnp.bfloat16
    sem = pltpu.SemaphoreType.DMA
    blocks = pl.pallas_call(
        fused_kernel,
        out_shape=jax.ShapeDtypeStruct((2 * PLANE, rows, columns), low),
        in_specs=[pl.BlockSpec(memory_space=pl.ANY)] * 6 + [pl.BlockSpec(memory_space=pltpu.SMEM)],
        out_specs=vmem,
        scratch_shapes=[
            pltpu.VMEM((rows, q_cols), low),
            pltpu.VMEM((held, kv_cols), low),
            pltpu.VMEM((held, kv_cols), low),
            pltpu.VMEM((rows, (REACH + 1) * rows), jnp.float32),
            pltpu.VMEM((PLANE, columns, q_cols), low),
            pltpu.VMEM((PLANE, rows, q_cols), low),
            pltpu.VMEM((2, PLANE, rows, columns), low),
            pltpu.VMEM((2, PLANE, rows, columns), low),
            pltpu.VMEM((2, PLANE, rows, columns), low),
            pltpu.VMEM((2, PLANE, rows, columns), low),
            sem((6,)), sem((4, 2)), sem((4, 2)), sem((4, 2)), sem((4, 2)),
            sem((REACH + 1, 2)), sem((REACH + 1, 2)),
            sem((2, 4)), sem((2, 4)),
            sem((kv_heads, 4)), sem((kv_heads, 4)),
            sem((2, PLANE)), sem((2, PLANE)), sem((2, PLANE)), sem((2, PLANE)),
        ],
        compiler_params=pltpu.CompilerParams(
            collective_id=0, has_side_effects=True, vmem_limit_bytes=60 * 1024 * 1024
        ),
        cost_estimate=pl.CostEstimate(
            flops=12_000_000_000, bytes_accessed=8_000_000, transcendentals=10_000_000
        ),
    )(
        queries, suffix_key_rows, suffix_value_rows, shared_prefix_keys, shared_prefix_values,
        out_weight.T, lengths,
    )
    return jnp.transpose(blocks, (1, 0, 2)).reshape(rows, 2 * PLANE * columns)


def solution(mesh):
    fused = mesh.shape["mp"] == 2 and mesh.shape["blk"] == PLANE * PLANE
    placed = (
        P("blk", "mp"),
        P("blk", "mp"),
        P("blk", "mp"),
        P("blk", "mp"),
        P("blk", "mp"),
        P("mp", "blk"),
        P(),
    )
    return jax.shard_map(
        per_device_fused if fused else per_device, mesh=mesh, in_specs=placed, out_specs=P("blk", "mp"), check_vma=False
    )
```

```python
import math

import jax
import jax.numpy as jnp
from jax import lax
from jax.experimental import pallas as pl
from jax.experimental.pallas import tpu as pltpu
from jax.sharding import PartitionSpec as P

HEAD_SIZE = 128


MASKED_SCORE = -1e30


def passed_along(block, axis, distance):
    devices = range(lax.axis_size(axis))
    route = [(i - distance, i) for i in devices if i - distance in devices]
    return lax.ppermute(block, axis, route)


def per_device(
    queries,
    suffix_key_rows,
    suffix_value_rows,
    shared_prefix_keys,
    shared_prefix_values,
    out_weight,
    lengths,
):
    tok_rows = queries.shape[0]
    kv_heads = suffix_key_rows.shape[1] // HEAD_SIZE
    q_heads = queries.shape[1] // HEAD_SIZE
    heads_per_group = q_heads // kv_heads
    blocks = lax.axis_size("blk")
    cycle_reach = blocks // 4
    my_block = lax.axis_index("blk")
    score_scale = 1.0 / math.sqrt(HEAD_SIZE)
    heads_of_query = queries.reshape(tok_rows, kv_heads, heads_per_group, HEAD_SIZE)
    req_ends = jnp.cumsum(lengths)
    local_rows = jnp.arange(tok_rows, dtype=jnp.int32)
    query_pos = my_block * tok_rows + local_rows

    def owner_of(position):
        return jnp.sum((position[:, None] >= req_ends[None, :]).astype(jnp.int32), axis=1)

    query_owner = owner_of(query_pos)

    def update(carry_state, key_block, value_block, visible):
        run_max, row_total, accumulated = carry_state
        count = key_block.shape[0]
        key_heads = key_block.reshape(count, kv_heads, HEAD_SIZE)
        value_heads = value_block.reshape(count, kv_heads, HEAD_SIZE)
        scores = (
            jnp.einsum(
                "qhgd,khd->hgqk", heads_of_query, key_heads, preferred_element_type=jnp.float32
            )
            * score_scale
        )
        if visible is not None:
            scores = jnp.where(visible[None, None], scores, MASKED_SCORE)
        new_max = jnp.maximum(run_max, jnp.max(scores, axis=-1))
        weights = jnp.exp(scores - new_max[..., None])
        if visible is not None:
            weights = jnp.where(visible[None, None], weights, 0.0)
        rescale = jnp.exp(run_max - new_max)
        row_total = row_total * rescale + jnp.sum(weights, axis=-1)
        contrib = jnp.einsum(
            "hgqk,khd->hgqd",
            weights.astype(jnp.bfloat16),
            value_heads,
            preferred_element_type=jnp.float32,
        )
        accumulated = accumulated * rescale[..., None] + contrib
        return (new_max, row_total, accumulated)

    start_state = (
        jnp.full((kv_heads, heads_per_group, tok_rows), MASKED_SCORE, jnp.float32),
        jnp.zeros((kv_heads, heads_per_group, tok_rows), jnp.float32),
        jnp.zeros((kv_heads, heads_per_group, tok_rows, HEAD_SIZE), jnp.float32),
    )
    carry_state = update(
        start_state,
        lax.all_gather(shared_prefix_keys, "blk", axis=0, tiled=True),
        lax.all_gather(shared_prefix_values, "blk", axis=0, tiled=True),
        None,
    )

    def visible_from(distance):
        key_pos = (my_block - distance) * tok_rows + local_rows
        key_owner = owner_of(key_pos)
        return (
            (key_owner[None, :] == query_owner[:, None])
            & (key_pos[None, :] <= query_pos[:, None])
            & (key_pos[None, :] >= 0)
        )

    kv_pair = jnp.stack((suffix_key_rows, suffix_value_rows))
    carry_state = update(carry_state, kv_pair[0], kv_pair[1], visible_from(0))

    def advance(distance, loop_carry):
        current, moving = loop_carry
        moving = passed_along(moving, "blk", 1)
        visible = visible_from(distance)
        current = update(current, moving[0], moving[1], visible)
        return (current, moving)

    carry_state, kv_pair = lax.fori_loop(1, cycle_reach + 1, advance, (carry_state, kv_pair))
    run_max, row_total, accumulated = carry_state
    attended = accumulated / row_total[..., None]
    attn = (
        jnp.transpose(attended, (2, 0, 1, 3))
        .reshape(tok_rows, q_heads * HEAD_SIZE)
        .astype(jnp.bfloat16)
    )
    product = jnp.dot(
        attn,
        lax.all_gather(out_weight, "blk", axis=1, tiled=True),
        preferred_element_type=jnp.float32,
    )
    return lax.psum_scatter(product.astype(jnp.bfloat16), "mp", scatter_dimension=1, tiled=True)


MESH = pl.DeviceIdType.MESH
NT = (((1,), (1,)), ((), ()))
REACH = 4
PLANE = 4
PIECES = 4


def fused_kernel(
    q_ref, k_ref, v_ref, pk_ref, pv_ref, w_ref, len_ref,
    out_ref,
    queries, keys, values, bias, weights, attn, mine, to_core, from_core, summed,
    local, pz_s, pz_r, pp_s, pp_r, sx_s, sx_r, w_s, w_r, at_s, at_r, mp_s, mp_r, out_s, out_r,
):
    rows = q_ref.shape[0]
    kv_heads = k_ref.shape[1] // HEAD_SIZE
    group = q_ref.shape[1] // k_ref.shape[1]
    part = pk_ref.shape[0]
    prefix = part * PLANE * PLANE
    chunk = part * PLANE
    me = lax.axis_index("blk")
    mp = lax.axis_index("mp")
    z = lax.div(me, PLANE)
    i = lax.rem(me, PLANE)
    z_hi, z_lo = lax.div(z, 2), lax.rem(z, 2)
    y, x = lax.div(i, 2), lax.rem(i, 2)
    x_mate = me + 1 - 2 * x
    y_mate = me + 2 * (1 - 2 * y)
    near = me + PLANE * (1 - 2 * z_lo)
    far = me + 2 * PLANE * (1 - 2 * z_hi)
    across = near + 1 - 2 * x
    shard = z_hi * 2 + y
    far_shard = (1 - z_hi) * 2 + y
    token = z_lo * 2 + x
    near_token = (1 - z_lo) * 2 + x
    x_token = z_lo * 2 + 1 - x

    def send(src, dst, send_sem, recv_sem, blk, core=None):
        return pltpu.make_async_remote_copy(
            src_ref=src, dst_ref=dst, send_sem=send_sem, recv_sem=recv_sem,
            device_id=(blk, mp if core is None else core), device_id_type=MESH,
        )

    def in_column(o):
        return lax.rem(z + o, PLANE) * PLANE + i

    def in_plane(o):
        return z * PLANE + lax.rem(i + o, PLANE)

    barrier = pltpu.get_barrier_semaphore()
    for o in (1, 2, 3):
        pl.semaphore_signal(barrier, inc=1, device_id=(in_column(o), mp), device_id_type=MESH)
        pl.semaphore_signal(barrier, inc=1, device_id=(in_plane(o), mp), device_id_type=MESH)
    pl.semaphore_signal(barrier, inc=1, device_id=(across, mp), device_id_type=MESH)
    pl.semaphore_signal(barrier, inc=1, device_id=(me, 1 - mp), device_id_type=MESH)

    own_rows = pl.ds(pl.multiple_of(i * chunk + z * part, part), part)
    own_copies = [
        pltpu.make_async_copy(source, target, local.at[n])
        for n, (source, target) in enumerate((
            (pk_ref, keys.at[own_rows]),
            (pv_ref, values.at[own_rows]),
            (k_ref, keys.at[pl.ds(prefix, rows)]),
            (v_ref, values.at[pl.ds(prefix, rows)]),
            (q_ref, queries),
            (w_ref, weights.at[shard]),
        ))
    ]
    for copy in own_copies:
        copy.start()
    pl.semaphore_wait(barrier, 8)

    kv = ((k_ref, pk_ref, keys), (v_ref, pv_ref, values))

    def suffix_rows(d):
        return pl.ds(prefix + d * rows, rows)

    def up_copy(c):
        own, _, held = kv[c]
        return send(own, held.at[suffix_rows(REACH)], sx_s.at[REACH, c], sx_r.at[REACH, c],
                    me + REACH)

    def prefix_up(o, c):
        _, own, held = kv[c]
        return send(own, held.at[own_rows], pz_s.at[o, c], pz_r.at[o, c], in_column(o))

    my_chunk = pl.ds(pl.multiple_of(i * chunk, chunk), chunk)

    def prefix_across(o, c):
        held = kv[c][2]
        return send(held.at[my_chunk], held.at[my_chunk], pp_s.at[o, c], pp_r.at[o, c],
                    in_plane(o))

    def across_own(d, c):
        own, _, held = kv[c]
        return send(own, held.at[suffix_rows(d)], sx_s.at[d, c], sx_r.at[d, c], in_plane(d))

    def across_relayed(d, c):
        held = kv[c][2]
        return send(held.at[suffix_rows(REACH)], held.at[suffix_rows(d)], sx_s.at[d, c],
                    sx_r.at[d, c], in_plane(d))

    piece = w_ref.shape[0] // PIECES

    def to_far(c):
        at = pl.ds(c * piece, piece)
        return send(w_ref.at[at], weights.at[shard, at], w_s.at[0, c], w_r.at[0, c], far)

    def to_y(c):
        at = pl.ds(c * piece, piece)
        return send(w_ref.at[at], weights.at[shard, at], w_s.at[1, c], w_r.at[1, c], y_mate)

    def far_to_y(c):
        block = weights.at[far_shard, pl.ds(c * piece, piece)]
        return send(block, block, w_s.at[2, c], w_r.at[2, c], y_mate)

    def pass_on(c):
        to_far(c).wait_recv()
        far_to_y(c).start()

    for o in (1, 2, 3):
        for c in (0, 1):
            prefix_up(o, c).start()

    @pl.when(z + 1 < PLANE)
    def _():
        up_copy(0).start()
        up_copy(1).start()

    for d in (1, 2, 3):
        @pl.when(i + d < PLANE)
        def _():
            across_own(d, 0).start()
            across_own(d, 1).start()

    for d in range(1, REACH + 1):
        @pl.when(me < d)
        def _():
            keys[suffix_rows(d), :] = jnp.zeros((rows, keys.shape[1]), keys.dtype)
            values[suffix_rows(d), :] = jnp.zeros((rows, keys.shape[1]), keys.dtype)

    query_pos = me * rows + lax.broadcasted_iota(jnp.int32, (rows, HEAD_SIZE), 0)
    first = jnp.zeros((rows, HEAD_SIZE), jnp.int32)
    end = jnp.int32(0)
    for r in range(len_ref.shape[0]):
        end = end + len_ref[r]
        first = jnp.maximum(first, jnp.where(query_pos >= end, end, 0))
    lane = lax.broadcasted_iota(jnp.int32, (rows, HEAD_SIZE), 1)
    for d in range(REACH + 1):
        for t in range(rows // HEAD_SIZE):
            key_pos = (me - d) * rows + t * HEAD_SIZE + lane
            seen = (key_pos >= first) & (key_pos <= query_pos)
            at = d * rows + t * HEAD_SIZE
            bias[:, at:at + HEAD_SIZE] = jnp.where(seen, 0.0, MASKED_SCORE)

    for copy in own_copies:
        copy.wait()
    for o in (1, 2, 3):
        for c in (0, 1):
            prefix_up(o, c).wait_recv()
    for o in (1, 2, 3):
        for c in (0, 1):
            prefix_across(o, c).start()

    @pl.when(z >= 1)
    def _():
        up_copy(0).wait_recv()
        up_copy(1).wait_recv()
        for d in (1, 2, 3):
            @pl.when(i + d >= PLANE)
            def _():
                across_relayed(d, 0).start()
                across_relayed(d, 1).start()

    for c in range(PIECES // 2):
        to_far(c).start()
    to_y(0).start()

    for o in (1, 2, 3):
        for c in (0, 1):
            prefix_across(o, c).wait_recv()
    for d in (1, 2, 3):
        @pl.when(me >= d)
        def _():
            across_own(d, 0).wait_recv()
            across_own(d, 1).wait_recv()
    for c in range(PIECES // 2, PIECES):
        to_far(c).start()
    for c in range(1, PIECES):
        to_y(c).start()

    exponent_scale = math.log2(math.e) / math.sqrt(HEAD_SIZE)
    width = group * HEAD_SIZE

    def attn_block(t, g):
        columns = pl.ds(pl.multiple_of(g * width, HEAD_SIZE), width)
        return attn.at[t, :, columns]

    def attn_to_x(g):
        block = attn_block(token, g)
        return send(block, block, at_s.at[g, 0], at_r.at[g, 0], x_mate)

    def attn_to_near(g):
        block = attn_block(token, g)
        return send(block, block, at_s.at[g, 1], at_r.at[g, 1], near)

    def near_to_x(g):
        block = attn_block(near_token, g)
        return send(block, block, at_s.at[g, 2], at_r.at[g, 2], x_mate)

    def x_to_near(g):
        block = attn_block(x_token, g)
        return send(block, block, at_s.at[g, 2], at_r.at[g, 2], near)

    def attn_pass_on(g):
        attn_to_x(g).wait_recv()
        attn_to_near(g).wait_recv()

        @pl.when(g != 1)
        def _():
            near_to_x(g).start()

        @pl.when(g == 1)
        def _():
            x_to_near(g).start()

    def one_group(g, carry):
        head = pl.ds(pl.multiple_of(g * HEAD_SIZE, HEAD_SIZE), HEAD_SIZE)
        for h in range(group):
            column = pl.ds(pl.multiple_of(g * width + h * HEAD_SIZE, HEAD_SIZE), HEAD_SIZE)
            q = queries[:, column]
            s_pre = lax.dot_general(q, keys[:prefix, head], NT, preferred_element_type=jnp.float32)
            s_suf = lax.dot_general(q, keys[prefix:, head], NT, preferred_element_type=jnp.float32)
            s_suf = s_suf + bias[...]
            peak = jnp.maximum(
                jnp.max(s_pre, axis=1, keepdims=True), jnp.max(s_suf, axis=1, keepdims=True)
            )
            p_pre = jnp.exp2((s_pre - peak) * exponent_scale)
            p_suf = jnp.exp2((s_suf - peak) * exponent_scale)
            total = jnp.sum(p_pre, axis=1, keepdims=True) + jnp.sum(p_suf, axis=1, keepdims=True)
            mixed = jnp.dot(
                p_pre.astype(jnp.bfloat16), values[:prefix, head],
                preferred_element_type=jnp.float32,
            ) + jnp.dot(
                p_suf.astype(jnp.bfloat16), values[prefix:, head],
                preferred_element_type=jnp.float32,
            )
            attn[token, :, column] = (mixed / total).astype(jnp.bfloat16)
        attn_to_x(g).start()
        attn_to_near(g).start()

        @pl.when(g >= 1)
        def _():
            attn_pass_on(g - 1)

        @pl.when(g == 1)
        def _():
            for c in range(PIECES // 2):
                pass_on(c)

        return carry

    lax.fori_loop(0, kv_heads, one_group, 0)
    attn_pass_on(jnp.int32(kv_heads - 1))
    for c in range(PIECES // 2, PIECES):
        pass_on(c)
    for c in range(PIECES):
        to_y(c).wait_recv()

    def to_sibling(low, t):
        return send(to_core.at[low, t], from_core.at[low, t], mp_s.at[low, t], mp_r.at[low, t],
                    me, 1 - mp)

    def member(t):
        return (z_hi * 2 + lax.div(t, 2)) * PLANE + y * 2 + lax.rem(t, 2)

    def column_block(t, low):
        return lax.div(t, 2) * PLANE + low * 2 + lax.rem(t, 2)

    def to_owner(low, t):
        return send(summed.at[low, t], out_ref.at[column_block(token, low)], out_s.at[low, t],
                    out_r.at[low, token], member(t))

    def out_arrival(low, t):
        return send(summed.at[low, t], out_ref.at[column_block(t, low)], out_s.at[low, t],
                    out_r.at[low, t], member(t))

    def shard_of(n):
        hi = z_hi + lax.div(n, 2) * (1 - 2 * z_hi)
        low = y + lax.rem(n, 2) * (1 - 2 * y)
        return hi * 2 + low, low, hi == mp

    def rows_from(o):
        lo = z_lo + lax.div(o, 2) * (1 - 2 * z_lo)
        return lo * 2 + x + lax.rem(o, 2) * (1 - 2 * x)

    def multiply(n, t):
        src, low, ours = shard_of(n)
        product = lax.dot_general(
            attn[t], weights[src], NT, preferred_element_type=jnp.float32
        ).astype(jnp.bfloat16)

        @pl.when(ours)
        def _():
            mine[low, t] = product

        @pl.when(jnp.logical_not(ours))
        def _():
            to_core[low, t] = product
            to_sibling(low, t).start()

    def add(n, t):
        src, low, ours = shard_of(n)

        @pl.when(ours)
        def _():
            to_sibling(low, t).wait_recv()
            both = mine[low, t].astype(jnp.float32) + from_core[low, t].astype(jnp.float32)
            both = both.astype(jnp.bfloat16)

            @pl.when(t == token)
            def _():
                out_ref[column_block(token, low)] = both

            @pl.when(t != token)
            def _():
                summed[low, t] = both
                to_owner(low, t).start()

    def one_source(o, carry):
        @pl.when(o == PLANE - 1)
        def _():
            for g in range(kv_heads):
                near_to_x(g).wait_recv()

        def times(n, c):
            multiply(n, rows_from(o))
            return c

        lax.fori_loop(0, PLANE - 1, times, 0)

        @pl.when(o >= 1)
        def _():
            def plus(n, c):
                add(n, rows_from(o - 1))
                return c

            lax.fori_loop(0, PLANE - 1, plus, 0)

        return carry

    lax.fori_loop(0, PLANE, one_source, 0)
    for n in range(PLANE - 1):
        add(jnp.int32(n), rows_from(PLANE - 1))

    for c in range(PIECES):
        far_to_y(c).wait_recv()

    def last_shard(o, carry):
        multiply(jnp.int32(PLANE - 1), rows_from(PLANE - 1 - o))

        @pl.when(o >= 1)
        def _():
            add(jnp.int32(PLANE - 1), rows_from(PLANE - o))

        return carry

    lax.fori_loop(0, PLANE, last_shard, 0)
    add(jnp.int32(PLANE - 1), rows_from(0))

    for low in (0, 1):
        for t in range(PLANE):
            to_sibling(low, t).wait_send()

            @pl.when(t != token)
            def _():
                out_arrival(low, t).wait_recv()
                out_arrival(low, t).wait_send()

    for o in (1, 2, 3):
        for c in (0, 1):
            prefix_up(o, c).wait_send()
            prefix_across(o, c).wait_send()
            across_own_sent = across_own(o, c)

            @pl.when((i + o < PLANE) | (z >= 1))
            def _():
                across_own_sent.wait_send()
    for c in (0, 1):
        @pl.when(z + 1 < PLANE)
        def _():
            up_copy(c).wait_send()
    for c in range(PIECES):
        to_far(c).wait_send()
        to_y(c).wait_send()
        far_to_y(c).wait_send()
    for g in range(kv_heads):
        attn_to_x(g).wait_send()
        attn_to_near(g).wait_send()
        near_to_x(g).wait_send()


def per_device_fused(
    queries,
    suffix_key_rows,
    suffix_value_rows,
    shared_prefix_keys,
    shared_prefix_values,
    out_weight,
    lengths,
):
    rows, q_cols = queries.shape
    kv_cols = suffix_key_rows.shape[1]
    columns = out_weight.shape[1]
    held = shared_prefix_keys.shape[0] * PLANE * PLANE + (REACH + 1) * rows
    kv_heads = kv_cols // HEAD_SIZE
    vmem = pl.BlockSpec(memory_space=pltpu.VMEM)
    low = jnp.bfloat16
    sem = pltpu.SemaphoreType.DMA
    blocks = pl.pallas_call(
        fused_kernel,
        out_shape=jax.ShapeDtypeStruct((2 * PLANE, rows, columns), low),
        in_specs=[pl.BlockSpec(memory_space=pl.ANY)] * 6 + [pl.BlockSpec(memory_space=pltpu.SMEM)],
        out_specs=vmem,
        scratch_shapes=[
            pltpu.VMEM((rows, q_cols), low),
            pltpu.VMEM((held, kv_cols), low),
            pltpu.VMEM((held, kv_cols), low),
            pltpu.VMEM((rows, (REACH + 1) * rows), jnp.float32),
            pltpu.VMEM((PLANE, columns, q_cols), low),
            pltpu.VMEM((PLANE, rows, q_cols), low),
            pltpu.VMEM((2, PLANE, rows, columns), low),
            pltpu.VMEM((2, PLANE, rows, columns), low),
            pltpu.VMEM((2, PLANE, rows, columns), low),
            pltpu.VMEM((2, PLANE, rows, columns), low),
            sem((6,)), sem((4, 2)), sem((4, 2)), sem((4, 2)), sem((4, 2)),
            sem((REACH + 1, 2)), sem((REACH + 1, 2)),
            sem((3, PIECES)), sem((3, PIECES)),
            sem((kv_heads, 3)), sem((kv_heads, 3)),
            sem((2, PLANE)), sem((2, PLANE)), sem((2, PLANE)), sem((2, PLANE)),
        ],
        compiler_params=pltpu.CompilerParams(
            collective_id=0, has_side_effects=True, vmem_limit_bytes=60 * 1024 * 1024
        ),
        cost_estimate=pl.CostEstimate(
            flops=12_000_000_000, bytes_accessed=8_000_000, transcendentals=10_000_000
        ),
    )(
        queries, suffix_key_rows, suffix_value_rows, shared_prefix_keys, shared_prefix_values,
        out_weight.T, lengths,
    )
    return jnp.transpose(blocks, (1, 0, 2)).reshape(rows, 2 * PLANE * columns)


def solution(mesh):
    fused = mesh.shape["mp"] == 2 and mesh.shape["blk"] == PLANE * PLANE
    placed = (
        P("blk", "mp"),
        P("blk", "mp"),
        P("blk", "mp"),
        P("blk", "mp"),
        P("blk", "mp"),
        P("mp", "blk"),
        P(),
    )
    return jax.shard_map(
        per_device_fused if fused else per_device, mesh=mesh, in_specs=placed, out_specs=P("blk", "mp"), check_vma=False
    )
```

```python
import math

import jax
import jax.numpy as jnp
from jax import lax
from jax.experimental import pallas as pl
from jax.experimental.pallas import tpu as pltpu
from jax.sharding import PartitionSpec as P

HEAD_SIZE = 128


MASKED_SCORE = -1e30


def passed_along(block, axis, distance):
    devices = range(lax.axis_size(axis))
    route = [(i - distance, i) for i in devices if i - distance in devices]
    return lax.ppermute(block, axis, route)


def per_device(
    queries,
    suffix_key_rows,
    suffix_value_rows,
    shared_prefix_keys,
    shared_prefix_values,
    out_weight,
    lengths,
):
    tok_rows = queries.shape[0]
    kv_heads = suffix_key_rows.shape[1] // HEAD_SIZE
    q_heads = queries.shape[1] // HEAD_SIZE
    heads_per_group = q_heads // kv_heads
    blocks = lax.axis_size("blk")
    cycle_reach = blocks // 4
    my_block = lax.axis_index("blk")
    score_scale = 1.0 / math.sqrt(HEAD_SIZE)
    heads_of_query = queries.reshape(tok_rows, kv_heads, heads_per_group, HEAD_SIZE)
    req_ends = jnp.cumsum(lengths)
    local_rows = jnp.arange(tok_rows, dtype=jnp.int32)
    query_pos = my_block * tok_rows + local_rows

    def owner_of(position):
        return jnp.sum((position[:, None] >= req_ends[None, :]).astype(jnp.int32), axis=1)

    query_owner = owner_of(query_pos)

    def update(carry_state, key_block, value_block, visible):
        run_max, row_total, accumulated = carry_state
        count = key_block.shape[0]
        key_heads = key_block.reshape(count, kv_heads, HEAD_SIZE)
        value_heads = value_block.reshape(count, kv_heads, HEAD_SIZE)
        scores = (
            jnp.einsum(
                "qhgd,khd->hgqk", heads_of_query, key_heads, preferred_element_type=jnp.float32
            )
            * score_scale
        )
        if visible is not None:
            scores = jnp.where(visible[None, None], scores, MASKED_SCORE)
        new_max = jnp.maximum(run_max, jnp.max(scores, axis=-1))
        weights = jnp.exp(scores - new_max[..., None])
        if visible is not None:
            weights = jnp.where(visible[None, None], weights, 0.0)
        rescale = jnp.exp(run_max - new_max)
        row_total = row_total * rescale + jnp.sum(weights, axis=-1)
        contrib = jnp.einsum(
            "hgqk,khd->hgqd",
            weights.astype(jnp.bfloat16),
            value_heads,
            preferred_element_type=jnp.float32,
        )
        accumulated = accumulated * rescale[..., None] + contrib
        return (new_max, row_total, accumulated)

    start_state = (
        jnp.full((kv_heads, heads_per_group, tok_rows), MASKED_SCORE, jnp.float32),
        jnp.zeros((kv_heads, heads_per_group, tok_rows), jnp.float32),
        jnp.zeros((kv_heads, heads_per_group, tok_rows, HEAD_SIZE), jnp.float32),
    )
    carry_state = update(
        start_state,
        lax.all_gather(shared_prefix_keys, "blk", axis=0, tiled=True),
        lax.all_gather(shared_prefix_values, "blk", axis=0, tiled=True),
        None,
    )

    def visible_from(distance):
        key_pos = (my_block - distance) * tok_rows + local_rows
        key_owner = owner_of(key_pos)
        return (
            (key_owner[None, :] == query_owner[:, None])
            & (key_pos[None, :] <= query_pos[:, None])
            & (key_pos[None, :] >= 0)
        )

    kv_pair = jnp.stack((suffix_key_rows, suffix_value_rows))
    carry_state = update(carry_state, kv_pair[0], kv_pair[1], visible_from(0))

    def advance(distance, loop_carry):
        current, moving = loop_carry
        moving = passed_along(moving, "blk", 1)
        visible = visible_from(distance)
        current = update(current, moving[0], moving[1], visible)
        return (current, moving)

    carry_state, kv_pair = lax.fori_loop(1, cycle_reach + 1, advance, (carry_state, kv_pair))
    run_max, row_total, accumulated = carry_state
    attended = accumulated / row_total[..., None]
    attn = (
        jnp.transpose(attended, (2, 0, 1, 3))
        .reshape(tok_rows, q_heads * HEAD_SIZE)
        .astype(jnp.bfloat16)
    )
    product = jnp.dot(
        attn,
        lax.all_gather(out_weight, "blk", axis=1, tiled=True),
        preferred_element_type=jnp.float32,
    )
    return lax.psum_scatter(product.astype(jnp.bfloat16), "mp", scatter_dimension=1, tiled=True)


MESH = pl.DeviceIdType.MESH
NT = (((1,), (1,)), ((), ()))
REACH = 4
PLANE = 4


def fused_kernel(
    q_ref, k_ref, v_ref, pk_ref, pv_ref, w_ref, len_ref,
    out_ref,
    queries, keys, values, bias, weights, attn, mine, to_core, from_core, summed,
    local, pz_s, pz_r, pp_s, pp_r, sx_s, sx_r, w_s, w_r, at_s, at_r, mp_s, mp_r, out_s, out_r,
):
    rows = q_ref.shape[0]
    kv_heads = k_ref.shape[1] // HEAD_SIZE
    group = q_ref.shape[1] // k_ref.shape[1]
    part = pk_ref.shape[0]
    prefix = part * PLANE * PLANE
    chunk = part * PLANE
    me = lax.axis_index("blk")
    mp = lax.axis_index("mp")
    z = lax.div(me, PLANE)
    i = lax.rem(me, PLANE)
    y, x = lax.div(i, 2), lax.rem(i, 2)
    x_mate = me + 1 - 2 * x
    y_mate = me + 2 * (1 - 2 * y)
    x_token = i + 1 - 2 * x
    y_token = i + 2 * (1 - 2 * y)

    def send(src, dst, send_sem, recv_sem, blk, core=None):
        return pltpu.make_async_remote_copy(
            src_ref=src, dst_ref=dst, send_sem=send_sem, recv_sem=recv_sem,
            device_id=(blk, mp if core is None else core), device_id_type=MESH,
        )

    def in_column(o):
        return lax.rem(z + o, PLANE) * PLANE + i

    def in_plane(o):
        return z * PLANE + lax.rem(i + o, PLANE)

    barrier = pltpu.get_barrier_semaphore()
    for o in (1, 2, 3):
        pl.semaphore_signal(barrier, inc=1, device_id=(in_column(o), mp), device_id_type=MESH)
        pl.semaphore_signal(barrier, inc=1, device_id=(in_plane(o), mp), device_id_type=MESH)
    pl.semaphore_signal(barrier, inc=1, device_id=(me, 1 - mp), device_id_type=MESH)

    own_rows = pl.ds(pl.multiple_of(i * chunk + z * part, part), part)
    own_copies = [
        pltpu.make_async_copy(source, target, local.at[n])
        for n, (source, target) in enumerate((
            (pk_ref, keys.at[own_rows]),
            (pv_ref, values.at[own_rows]),
            (k_ref, keys.at[pl.ds(prefix, rows)]),
            (v_ref, values.at[pl.ds(prefix, rows)]),
            (q_ref, queries),
            (w_ref, weights.at[z]),
        ))
    ]
    for copy in own_copies:
        copy.start()
    pl.semaphore_wait(barrier, 7)

    kv = ((k_ref, pk_ref, keys), (v_ref, pv_ref, values))

    def suffix_rows(d):
        return pl.ds(prefix + d * rows, rows)

    def up_copy(c):
        own, _, held = kv[c]
        return send(own, held.at[suffix_rows(REACH)], sx_s.at[REACH, c], sx_r.at[REACH, c],
                    me + REACH)

    def prefix_up(o, c):
        _, own, held = kv[c]
        return send(own, held.at[own_rows], pz_s.at[o, c], pz_r.at[o, c], in_column(o))

    my_chunk = pl.ds(pl.multiple_of(i * chunk, chunk), chunk)

    def prefix_across(o, c):
        held = kv[c][2]
        return send(held.at[my_chunk], held.at[my_chunk], pp_s.at[o, c], pp_r.at[o, c],
                    in_plane(o))

    def across_own(d, c):
        own, _, held = kv[c]
        return send(own, held.at[suffix_rows(d)], sx_s.at[d, c], sx_r.at[d, c], in_plane(d))

    def across_relayed(d, c):
        held = kv[c][2]
        return send(held.at[suffix_rows(REACH)], held.at[suffix_rows(d)], sx_s.at[d, c],
                    sx_r.at[d, c], in_plane(d))

    def weight_hop(way, k):
        origin = z - (k - 1) if way == 0 else z + (k - 1)
        to = me + PLANE if way == 0 else me - PLANE
        source = w_ref if k == 1 else weights.at[origin]
        return send(source, weights.at[origin], w_s.at[way, k], w_r.at[way, k], to)

    def sends_hop(way, k):
        if way == 0:
            return (z - (k - 1) >= 0) & (z + 1 < PLANE)
        return (z + (k - 1) < PLANE) & (z >= 1)

    def gets_hop(way, k):
        return z - k >= 0 if way == 0 else z + k < PLANE

    def start_hop(k):
        for way in (0, 1):
            @pl.when(sends_hop(way, k))
            def _():
                weight_hop(way, k).start()

    def take_hop(k):
        for way in (0, 1):
            @pl.when(gets_hop(way, k))
            def _():
                weight_hop(way, k).wait_recv()

    for o in (1, 2, 3):
        for c in (0, 1):
            prefix_up(o, c).start()

    @pl.when(z + 1 < PLANE)
    def _():
        up_copy(0).start()
        up_copy(1).start()

    for d in (1, 2, 3):
        @pl.when(i + d < PLANE)
        def _():
            across_own(d, 0).start()
            across_own(d, 1).start()

    for d in range(1, REACH + 1):
        @pl.when(me < d)
        def _():
            keys[suffix_rows(d), :] = jnp.zeros((rows, keys.shape[1]), keys.dtype)
            values[suffix_rows(d), :] = jnp.zeros((rows, keys.shape[1]), keys.dtype)

    query_pos = me * rows + lax.broadcasted_iota(jnp.int32, (rows, HEAD_SIZE), 0)
    first = jnp.zeros((rows, HEAD_SIZE), jnp.int32)
    end = jnp.int32(0)
    for r in range(len_ref.shape[0]):
        end = end + len_ref[r]
        first = jnp.maximum(first, jnp.where(query_pos >= end, end, 0))
    lane = lax.broadcasted_iota(jnp.int32, (rows, HEAD_SIZE), 1)
    for d in range(REACH + 1):
        for t in range(rows // HEAD_SIZE):
            key_pos = (me - d) * rows + t * HEAD_SIZE + lane
            seen = (key_pos >= first) & (key_pos <= query_pos)
            at = d * rows + t * HEAD_SIZE
            bias[:, at:at + HEAD_SIZE] = jnp.where(seen, 0.0, MASKED_SCORE)

    for copy in own_copies:
        copy.wait()
    for o in (1, 2, 3):
        for c in (0, 1):
            prefix_up(o, c).wait_recv()
    for o in (1, 2, 3):
        for c in (0, 1):
            prefix_across(o, c).start()

    @pl.when(z >= 1)
    def _():
        up_copy(0).wait_recv()
        up_copy(1).wait_recv()
        for d in (1, 2, 3):
            @pl.when(i + d >= PLANE)
            def _():
                across_relayed(d, 0).start()
                across_relayed(d, 1).start()

    @pl.when(z + 1 < PLANE)
    def _():
        up_copy(0).wait_send()
        up_copy(1).wait_send()

    start_hop(1)

    for o in (1, 2, 3):
        for c in (0, 1):
            prefix_across(o, c).wait_recv()
    for d in (1, 2, 3):
        @pl.when(me >= d)
        def _():
            across_own(d, 0).wait_recv()
            across_own(d, 1).wait_recv()

    exponent_scale = math.log2(math.e) / math.sqrt(HEAD_SIZE)
    width = group * HEAD_SIZE

    def attn_block(t, g):
        columns = pl.ds(pl.multiple_of(g * width, HEAD_SIZE), width)
        return attn.at[t, :, columns]

    def attn_to_x(g):
        block = attn_block(i, g)
        return send(block, block, at_s.at[g, 0], at_r.at[g, 0], x_mate)

    def attn_to_y(g):
        block = attn_block(i, g)
        return send(block, block, at_s.at[g, 1], at_r.at[g, 1], y_mate)

    def y_to_x(g):
        block = attn_block(y_token, g)
        return send(block, block, at_s.at[g, 2], at_r.at[g, 2], x_mate)

    def x_to_y(g):
        block = attn_block(x_token, g)
        return send(block, block, at_s.at[g, 2], at_r.at[g, 2], y_mate)

    def attn_pass_on(g):
        attn_to_x(g).wait_recv()
        attn_to_y(g).wait_recv()

        @pl.when(lax.rem(g, 2) == 0)
        def _():
            y_to_x(g).start()

        @pl.when(lax.rem(g, 2) == 1)
        def _():
            x_to_y(g).start()

    def one_group(g, carry):
        head = pl.ds(pl.multiple_of(g * HEAD_SIZE, HEAD_SIZE), HEAD_SIZE)
        for h in range(group):
            column = pl.ds(pl.multiple_of(g * width + h * HEAD_SIZE, HEAD_SIZE), HEAD_SIZE)
            q = queries[:, column]
            s_pre = lax.dot_general(q, keys[:prefix, head], NT, preferred_element_type=jnp.float32)
            s_suf = lax.dot_general(q, keys[prefix:, head], NT, preferred_element_type=jnp.float32)
            s_suf = s_suf + bias[...]
            peak = jnp.maximum(
                jnp.max(s_pre, axis=1, keepdims=True), jnp.max(s_suf, axis=1, keepdims=True)
            )
            p_pre = jnp.exp2((s_pre - peak) * exponent_scale)
            p_suf = jnp.exp2((s_suf - peak) * exponent_scale)
            total = jnp.sum(p_pre, axis=1, keepdims=True) + jnp.sum(p_suf, axis=1, keepdims=True)
            mixed = jnp.dot(
                p_pre.astype(jnp.bfloat16), values[:prefix, head],
                preferred_element_type=jnp.float32,
            ) + jnp.dot(
                p_suf.astype(jnp.bfloat16), values[prefix:, head],
                preferred_element_type=jnp.float32,
            )
            attn[i, :, column] = (mixed / total).astype(jnp.bfloat16)
        attn_to_x(g).start()
        attn_to_y(g).start()

        @pl.when(g == 0)
        def _():
            take_hop(1)
            start_hop(2)

        @pl.when(g >= 1)
        def _():
            attn_pass_on(g - 1)

        return carry

    lax.fori_loop(0, kv_heads, one_group, 0)

    take_hop(2)
    start_hop(3)
    attn_pass_on(jnp.int32(kv_heads - 1))

    def to_sibling(low, t):
        return send(to_core.at[low, t], from_core.at[low, t], mp_s.at[low, t], mp_r.at[low, t],
                    me, 1 - mp)

    def to_owner(low, t):
        return send(summed.at[low, t], out_ref.at[low * PLANE + i], out_s.at[low, t],
                    out_r.at[low, i], z * PLANE + t)

    def out_arrival(low, t):
        return send(summed.at[low, t], out_ref.at[low * PLANE + t], out_s.at[low, t],
                    out_r.at[low, t], z * PLANE + t)

    def shard(n):
        inner = lax.div(z * (3 - z), 2)
        f = n + inner * (1 - 2 * n) * (1 - lax.div(n, 2))
        src = f + lax.div(z, 2) * (3 - 2 * f)
        return src, lax.rem(src, 2), lax.div(src, 2) == mp

    def rows_from(o):
        return (y + lax.div(o, 2) * (1 - 2 * y)) * 2 + x + lax.rem(o, 2) * (1 - 2 * x)

    def multiply(n, t):
        src, low, ours = shard(n)
        product = lax.dot_general(
            attn[t], weights[src], NT, preferred_element_type=jnp.float32
        ).astype(jnp.bfloat16)

        @pl.when(ours)
        def _():
            mine[low, t] = product

        @pl.when(jnp.logical_not(ours))
        def _():
            to_core[low, t] = product
            to_sibling(low, t).start()

    def add(n, t):
        src, low, ours = shard(n)

        @pl.when(ours)
        def _():
            to_sibling(low, t).wait_recv()
            both = mine[low, t].astype(jnp.float32) + from_core[low, t].astype(jnp.float32)
            both = both.astype(jnp.bfloat16)

            @pl.when(t == i)
            def _():
                out_ref[low * PLANE + i] = both

            @pl.when(t != i)
            def _():
                summed[low, t] = both
                to_owner(low, t).start()

    def one_source(o, carry):
        @pl.when(o == PLANE - 1)
        def _():
            for g in range(kv_heads):
                y_to_x(g).wait_recv()

        def times(n, c):
            multiply(n, rows_from(o))
            return c

        lax.fori_loop(0, PLANE - 1, times, 0)

        @pl.when(o >= 1)
        def _():
            def plus(n, c):
                add(n, rows_from(o - 1))
                return c

            lax.fori_loop(0, PLANE - 1, plus, 0)

        return carry

    lax.fori_loop(0, PLANE, one_source, 0)
    for n in range(PLANE - 1):
        add(jnp.int32(n), rows_from(PLANE - 1))

    take_hop(3)

    def last_shard(o, carry):
        multiply(jnp.int32(PLANE - 1), rows_from(PLANE - 1 - o))

        @pl.when(o >= 1)
        def _():
            add(jnp.int32(PLANE - 1), rows_from(PLANE - o))

        return carry

    lax.fori_loop(0, PLANE, last_shard, 0)
    add(jnp.int32(PLANE - 1), rows_from(0))

    for low in (0, 1):
        for t in range(PLANE):
            to_sibling(low, t).wait_send()

            @pl.when(t != i)
            def _():
                out_arrival(low, t).wait_recv()
                out_arrival(low, t).wait_send()

    for o in (1, 2, 3):
        for c in (0, 1):
            prefix_up(o, c).wait_send()
            prefix_across(o, c).wait_send()
            across_own_sent = across_own(o, c)

            @pl.when((i + o < PLANE) | (z >= 1))
            def _():
                across_own_sent.wait_send()
    for g in range(kv_heads):
        attn_to_x(g).wait_send()
        attn_to_y(g).wait_send()
        y_to_x(g).wait_send()
    for k in (1, 2, 3):
        for way in (0, 1):
            @pl.when(sends_hop(way, k))
            def _():
                weight_hop(way, k).wait_send()


def per_device_fused(
    queries,
    suffix_key_rows,
    suffix_value_rows,
    shared_prefix_keys,
    shared_prefix_values,
    out_weight,
    lengths,
):
    rows, q_cols = queries.shape
    kv_cols = suffix_key_rows.shape[1]
    columns = out_weight.shape[1]
    held = shared_prefix_keys.shape[0] * PLANE * PLANE + (REACH + 1) * rows
    kv_heads = kv_cols // HEAD_SIZE
    vmem = pl.BlockSpec(memory_space=pltpu.VMEM)
    low = jnp.bfloat16
    sem = pltpu.SemaphoreType.DMA
    blocks = pl.pallas_call(
        fused_kernel,
        out_shape=jax.ShapeDtypeStruct((2 * PLANE, rows, columns), low),
        in_specs=[pl.BlockSpec(memory_space=pl.ANY)] * 6 + [pl.BlockSpec(memory_space=pltpu.SMEM)],
        out_specs=vmem,
        scratch_shapes=[
            pltpu.VMEM((rows, q_cols), low),
            pltpu.VMEM((held, kv_cols), low),
            pltpu.VMEM((held, kv_cols), low),
            pltpu.VMEM((rows, (REACH + 1) * rows), jnp.float32),
            pltpu.VMEM((PLANE, columns, q_cols), low),
            pltpu.VMEM((PLANE, rows, q_cols), low),
            pltpu.VMEM((2, PLANE, rows, columns), low),
            pltpu.VMEM((2, PLANE, rows, columns), low),
            pltpu.VMEM((2, PLANE, rows, columns), low),
            pltpu.VMEM((2, PLANE, rows, columns), low),
            sem((6,)), sem((4, 2)), sem((4, 2)), sem((4, 2)), sem((4, 2)),
            sem((REACH + 1, 2)), sem((REACH + 1, 2)),
            sem((2, 4)), sem((2, 4)),
            sem((kv_heads, 3)), sem((kv_heads, 3)),
            sem((2, PLANE)), sem((2, PLANE)), sem((2, PLANE)), sem((2, PLANE)),
        ],
        compiler_params=pltpu.CompilerParams(
            collective_id=0, has_side_effects=True, vmem_limit_bytes=60 * 1024 * 1024
        ),
        cost_estimate=pl.CostEstimate(
            flops=12_000_000_000, bytes_accessed=8_000_000, transcendentals=10_000_000
        ),
    )(
        queries, suffix_key_rows, suffix_value_rows, shared_prefix_keys, shared_prefix_values,
        out_weight.T, lengths,
    )
    return jnp.transpose(blocks, (1, 0, 2)).reshape(rows, 2 * PLANE * columns)


def solution(mesh):
    fused = mesh.shape["mp"] == 2 and mesh.shape["blk"] == PLANE * PLANE
    placed = (
        P("blk", "mp"),
        P("blk", "mp"),
        P("blk", "mp"),
        P("blk", "mp"),
        P("blk", "mp"),
        P("mp", "blk"),
        P(),
    )
    return jax.shard_map(
        per_device_fused if fused else per_device, mesh=mesh, in_specs=placed, out_specs=P("blk", "mp"), check_vma=False
    )
```

```python
import math

import jax
import jax.numpy as jnp
from jax import lax
from jax.experimental import pallas as pl
from jax.experimental.pallas import tpu as pltpu
from jax.sharding import PartitionSpec as P

HEAD_SIZE = 128


MASKED_SCORE = -1e30


def passed_along(block, axis, distance):
    devices = range(lax.axis_size(axis))
    route = [(i - distance, i) for i in devices if i - distance in devices]
    return lax.ppermute(block, axis, route)


def per_device(
    queries,
    suffix_key_rows,
    suffix_value_rows,
    shared_prefix_keys,
    shared_prefix_values,
    out_weight,
    lengths,
):
    tok_rows = queries.shape[0]
    kv_heads = suffix_key_rows.shape[1] // HEAD_SIZE
    q_heads = queries.shape[1] // HEAD_SIZE
    heads_per_group = q_heads // kv_heads
    blocks = lax.axis_size("blk")
    cycle_reach = blocks // 4
    my_block = lax.axis_index("blk")
    score_scale = 1.0 / math.sqrt(HEAD_SIZE)
    heads_of_query = queries.reshape(tok_rows, kv_heads, heads_per_group, HEAD_SIZE)
    req_ends = jnp.cumsum(lengths)
    local_rows = jnp.arange(tok_rows, dtype=jnp.int32)
    query_pos = my_block * tok_rows + local_rows

    def owner_of(position):
        return jnp.sum((position[:, None] >= req_ends[None, :]).astype(jnp.int32), axis=1)

    query_owner = owner_of(query_pos)

    def update(carry_state, key_block, value_block, visible):
        run_max, row_total, accumulated = carry_state
        count = key_block.shape[0]
        key_heads = key_block.reshape(count, kv_heads, HEAD_SIZE)
        value_heads = value_block.reshape(count, kv_heads, HEAD_SIZE)
        scores = (
            jnp.einsum(
                "qhgd,khd->hgqk", heads_of_query, key_heads, preferred_element_type=jnp.float32
            )
            * score_scale
        )
        if visible is not None:
            scores = jnp.where(visible[None, None], scores, MASKED_SCORE)
        new_max = jnp.maximum(run_max, jnp.max(scores, axis=-1))
        weights = jnp.exp(scores - new_max[..., None])
        if visible is not None:
            weights = jnp.where(visible[None, None], weights, 0.0)
        rescale = jnp.exp(run_max - new_max)
        row_total = row_total * rescale + jnp.sum(weights, axis=-1)
        contrib = jnp.einsum(
            "hgqk,khd->hgqd",
            weights.astype(jnp.bfloat16),
            value_heads,
            preferred_element_type=jnp.float32,
        )
        accumulated = accumulated * rescale[..., None] + contrib
        return (new_max, row_total, accumulated)

    start_state = (
        jnp.full((kv_heads, heads_per_group, tok_rows), MASKED_SCORE, jnp.float32),
        jnp.zeros((kv_heads, heads_per_group, tok_rows), jnp.float32),
        jnp.zeros((kv_heads, heads_per_group, tok_rows, HEAD_SIZE), jnp.float32),
    )
    carry_state = update(
        start_state,
        lax.all_gather(shared_prefix_keys, "blk", axis=0, tiled=True),
        lax.all_gather(shared_prefix_values, "blk", axis=0, tiled=True),
        None,
    )

    def visible_from(distance):
        key_pos = (my_block - distance) * tok_rows + local_rows
        key_owner = owner_of(key_pos)
        return (
            (key_owner[None, :] == query_owner[:, None])
            & (key_pos[None, :] <= query_pos[:, None])
            & (key_pos[None, :] >= 0)
        )

    kv_pair = jnp.stack((suffix_key_rows, suffix_value_rows))
    carry_state = update(carry_state, kv_pair[0], kv_pair[1], visible_from(0))

    def advance(distance, loop_carry):
        current, moving = loop_carry
        moving = passed_along(moving, "blk", 1)
        visible = visible_from(distance)
        current = update(current, moving[0], moving[1], visible)
        return (current, moving)

    carry_state, kv_pair = lax.fori_loop(1, cycle_reach + 1, advance, (carry_state, kv_pair))
    run_max, row_total, accumulated = carry_state
    attended = accumulated / row_total[..., None]
    attn = (
        jnp.transpose(attended, (2, 0, 1, 3))
        .reshape(tok_rows, q_heads * HEAD_SIZE)
        .astype(jnp.bfloat16)
    )
    product = jnp.dot(
        attn,
        lax.all_gather(out_weight, "blk", axis=1, tiled=True),
        preferred_element_type=jnp.float32,
    )
    return lax.psum_scatter(product.astype(jnp.bfloat16), "mp", scatter_dimension=1, tiled=True)


MESH = pl.DeviceIdType.MESH
NT = (((1,), (1,)), ((), ()))
REACH = 4
PLANE = 4


def fused_kernel(
    q_ref, k_ref, v_ref, pk_ref, pv_ref, w_ref, len_ref,
    out_ref,
    queries, keys, values, bias, weights, attn, mine, to_core, from_core, summed,
    local, pz_s, pz_r, pp_s, pp_r, sx_s, sx_r, w_s, w_r, at_s, at_r, mp_s, mp_r, out_s, out_r,
):
    rows = q_ref.shape[0]
    kv_heads = k_ref.shape[1] // HEAD_SIZE
    group = q_ref.shape[1] // k_ref.shape[1]
    part = pk_ref.shape[0]
    prefix = part * PLANE * PLANE
    chunk = part * PLANE
    me = lax.axis_index("blk")
    mp = lax.axis_index("mp")
    z = lax.div(me, PLANE)
    i = lax.rem(me, PLANE)
    y, x = lax.div(i, 2), lax.rem(i, 2)
    x_mate = me + 1 - 2 * x
    y_mate = me + 2 * (1 - 2 * y)
    x_token = i + 1 - 2 * x
    y_token = i + 2 * (1 - 2 * y)

    def send(src, dst, send_sem, recv_sem, blk, core=None):
        return pltpu.make_async_remote_copy(
            src_ref=src, dst_ref=dst, send_sem=send_sem, recv_sem=recv_sem,
            device_id=(blk, mp if core is None else core), device_id_type=MESH,
        )

    def in_column(o):
        return lax.rem(z + o, PLANE) * PLANE + i

    def in_plane(o):
        return z * PLANE + lax.rem(i + o, PLANE)

    barrier = pltpu.get_barrier_semaphore()
    for o in (1, 2, 3):
        pl.semaphore_signal(barrier, inc=1, device_id=(in_column(o), mp), device_id_type=MESH)
        pl.semaphore_signal(barrier, inc=1, device_id=(in_plane(o), mp), device_id_type=MESH)
    pl.semaphore_signal(barrier, inc=1, device_id=(me, 1 - mp), device_id_type=MESH)

    own_rows = pl.ds(pl.multiple_of(i * chunk + z * part, part), part)
    own_copies = [
        pltpu.make_async_copy(source, target, local.at[n])
        for n, (source, target) in enumerate((
            (pk_ref, keys.at[own_rows]),
            (pv_ref, values.at[own_rows]),
            (k_ref, keys.at[pl.ds(prefix, rows)]),
            (v_ref, values.at[pl.ds(prefix, rows)]),
            (q_ref, queries),
            (w_ref, weights.at[z]),
        ))
    ]
    for copy in own_copies:
        copy.start()
    pl.semaphore_wait(barrier, 7)

    kv = ((k_ref, pk_ref, keys), (v_ref, pv_ref, values))

    def suffix_rows(d):
        return pl.ds(prefix + d * rows, rows)

    def up_copy(c):
        own, _, held = kv[c]
        return send(own, held.at[suffix_rows(REACH)], sx_s.at[REACH, c], sx_r.at[REACH, c],
                    me + REACH)

    def prefix_up(o, c):
        _, own, held = kv[c]
        return send(own, held.at[own_rows], pz_s.at[o, c], pz_r.at[o, c], in_column(o))

    my_chunk = pl.ds(pl.multiple_of(i * chunk, chunk), chunk)

    def prefix_across(o, c):
        held = kv[c][2]
        return send(held.at[my_chunk], held.at[my_chunk], pp_s.at[o, c], pp_r.at[o, c],
                    in_plane(o))

    def across_own(d, c):
        own, _, held = kv[c]
        return send(own, held.at[suffix_rows(d)], sx_s.at[d, c], sx_r.at[d, c], in_plane(d))

    def across_relayed(d, c):
        held = kv[c][2]
        return send(held.at[suffix_rows(REACH)], held.at[suffix_rows(d)], sx_s.at[d, c],
                    sx_r.at[d, c], in_plane(d))

    def weight_hop(way, k):
        origin = z - (k - 1) if way == 0 else z + (k - 1)
        to = me + PLANE if way == 0 else me - PLANE
        source = w_ref if k == 1 else weights.at[origin]
        return send(source, weights.at[origin], w_s.at[way, k], w_r.at[way, k], to)

    def sends_hop(way, k):
        if way == 0:
            return (z - (k - 1) >= 0) & (z + 1 < PLANE)
        return (z + (k - 1) < PLANE) & (z >= 1)

    def gets_hop(way, k):
        return z - k >= 0 if way == 0 else z + k < PLANE

    def start_hop(k):
        for way in (0, 1):
            @pl.when(sends_hop(way, k))
            def _():
                weight_hop(way, k).start()

    def take_hop(k):
        for way in (0, 1):
            @pl.when(gets_hop(way, k))
            def _():
                weight_hop(way, k).wait_recv()

    for o in (1, 2, 3):
        for c in (0, 1):
            prefix_up(o, c).start()

    @pl.when(z + 1 < PLANE)
    def _():
        up_copy(0).start()
        up_copy(1).start()

    for d in (1, 2, 3):
        @pl.when(i + d < PLANE)
        def _():
            across_own(d, 0).start()
            across_own(d, 1).start()

    for d in range(1, REACH + 1):
        @pl.when(me < d)
        def _():
            keys[suffix_rows(d), :] = jnp.zeros((rows, keys.shape[1]), keys.dtype)
            values[suffix_rows(d), :] = jnp.zeros((rows, keys.shape[1]), keys.dtype)

    query_pos = me * rows + lax.broadcasted_iota(jnp.int32, (rows, HEAD_SIZE), 0)
    first = jnp.zeros((rows, HEAD_SIZE), jnp.int32)
    end = jnp.int32(0)
    for r in range(len_ref.shape[0]):
        end = end + len_ref[r]
        first = jnp.maximum(first, jnp.where(query_pos >= end, end, 0))
    lane = lax.broadcasted_iota(jnp.int32, (rows, HEAD_SIZE), 1)
    for d in range(REACH + 1):
        for t in range(rows // HEAD_SIZE):
            key_pos = (me - d) * rows + t * HEAD_SIZE + lane
            seen = (key_pos >= first) & (key_pos <= query_pos)
            at = d * rows + t * HEAD_SIZE
            bias[:, at:at + HEAD_SIZE] = jnp.where(seen, 0.0, MASKED_SCORE)

    for copy in own_copies:
        copy.wait()
    for o in (1, 2, 3):
        for c in (0, 1):
            prefix_up(o, c).wait_recv()
    for o in (1, 2, 3):
        for c in (0, 1):
            prefix_across(o, c).start()

    @pl.when(z >= 1)
    def _():
        up_copy(0).wait_recv()
        up_copy(1).wait_recv()
        for d in (1, 2, 3):
            @pl.when(i + d >= PLANE)
            def _():
                across_relayed(d, 0).start()
                across_relayed(d, 1).start()

    @pl.when(z + 1 < PLANE)
    def _():
        up_copy(0).wait_send()
        up_copy(1).wait_send()

    start_hop(1)

    for o in (1, 2, 3):
        for c in (0, 1):
            prefix_across(o, c).wait_recv()
    for d in (1, 2, 3):
        @pl.when(me >= d)
        def _():
            across_own(d, 0).wait_recv()
            across_own(d, 1).wait_recv()

    exponent_scale = math.log2(math.e) / math.sqrt(HEAD_SIZE)
    width = group * HEAD_SIZE

    def attn_block(t, g):
        columns = pl.ds(pl.multiple_of(g * width, HEAD_SIZE), width)
        return attn.at[t, :, columns]

    def attn_to_x(g):
        block = attn_block(i, g)
        return send(block, block, at_s.at[g, 0], at_r.at[g, 0], x_mate)

    def attn_to_y(g):
        block = attn_block(i, g)
        return send(block, block, at_s.at[g, 1], at_r.at[g, 1], y_mate)

    def y_to_x(g):
        block = attn_block(y_token, g)
        return send(block, block, at_s.at[g, 2], at_r.at[g, 2], x_mate)

    def x_to_y(g):
        block = attn_block(x_token, g)
        return send(block, block, at_s.at[g, 2], at_r.at[g, 2], y_mate)

    def attn_pass_on(g):
        attn_to_x(g).wait_recv()
        attn_to_y(g).wait_recv()

        @pl.when(lax.rem(g, 2) == 0)
        def _():
            y_to_x(g).start()

        @pl.when(lax.rem(g, 2) == 1)
        def _():
            x_to_y(g).start()

    def one_group(g, carry):
        head = pl.ds(pl.multiple_of(g * HEAD_SIZE, HEAD_SIZE), HEAD_SIZE)
        for h in range(group):
            column = pl.ds(pl.multiple_of(g * width + h * HEAD_SIZE, HEAD_SIZE), HEAD_SIZE)
            q = queries[:, column]
            s_pre = lax.dot_general(q, keys[:prefix, head], NT, preferred_element_type=jnp.float32)
            s_suf = lax.dot_general(q, keys[prefix:, head], NT, preferred_element_type=jnp.float32)
            s_suf = s_suf + bias[...]
            peak = jnp.maximum(
                jnp.max(s_pre, axis=1, keepdims=True), jnp.max(s_suf, axis=1, keepdims=True)
            )
            p_pre = jnp.exp2((s_pre - peak) * exponent_scale)
            p_suf = jnp.exp2((s_suf - peak) * exponent_scale)
            total = jnp.sum(p_pre, axis=1, keepdims=True) + jnp.sum(p_suf, axis=1, keepdims=True)
            mixed = jnp.dot(
                p_pre.astype(jnp.bfloat16), values[:prefix, head],
                preferred_element_type=jnp.float32,
            ) + jnp.dot(
                p_suf.astype(jnp.bfloat16), values[prefix:, head],
                preferred_element_type=jnp.float32,
            )
            attn[i, :, column] = (mixed / total).astype(jnp.bfloat16)
        attn_to_x(g).start()
        attn_to_y(g).start()

        @pl.when(g == 0)
        def _():
            take_hop(1)
            start_hop(2)

        @pl.when(g >= 1)
        def _():
            attn_pass_on(g - 1)

        return carry

    lax.fori_loop(0, kv_heads, one_group, 0)

    take_hop(2)
    start_hop(3)
    attn_pass_on(jnp.int32(kv_heads - 1))

    def to_sibling(low, t):
        return send(to_core.at[low, t], from_core.at[low, t], mp_s.at[low, t], mp_r.at[low, t],
                    me, 1 - mp)

    def to_owner(low, t):
        return send(summed.at[low, t], out_ref.at[low * PLANE + i], out_s.at[low, t],
                    out_r.at[low, i], z * PLANE + t)

    def out_arrival(low, t):
        return send(summed.at[low, t], out_ref.at[low * PLANE + t], out_s.at[low, t],
                    out_r.at[low, t], z * PLANE + t)

    def shard(n):
        inner = lax.div(z * (3 - z), 2)
        f = n + inner * (1 - 2 * n) * (1 - lax.div(n, 2))
        src = f + lax.div(z, 2) * (3 - 2 * f)
        return src, lax.rem(src, 2), lax.div(src, 2) == mp

    def rows_from(o):
        return (y + lax.div(o, 2) * (1 - 2 * y)) * 2 + x + lax.rem(o, 2) * (1 - 2 * x)

    def multiply(n, t):
        src, low, ours = shard(n)
        product = lax.dot_general(
            attn[t], weights[src], NT, preferred_element_type=jnp.float32
        ).astype(jnp.bfloat16)

        @pl.when(ours)
        def _():
            mine[low, t] = product

        @pl.when(jnp.logical_not(ours))
        def _():
            to_core[low, t] = product
            to_sibling(low, t).start()

    def add(n, t):
        src, low, ours = shard(n)

        @pl.when(ours)
        def _():
            to_sibling(low, t).wait_recv()
            both = mine[low, t].astype(jnp.float32) + from_core[low, t].astype(jnp.float32)
            both = both.astype(jnp.bfloat16)

            @pl.when(t == i)
            def _():
                out_ref[low * PLANE + i] = both

            @pl.when(t != i)
            def _():
                summed[low, t] = both
                to_owner(low, t).start()

    def one_source(o, carry):
        @pl.when(o == PLANE - 1)
        def _():
            for g in range(kv_heads):
                y_to_x(g).wait_recv()

        def times(n, c):
            multiply(n, rows_from(o))
            return c

        lax.fori_loop(0, PLANE - 1, times, 0)

        @pl.when(o >= 1)
        def _():
            def plus(n, c):
                add(n, rows_from(o - 1))
                return c

            lax.fori_loop(0, PLANE - 1, plus, 0)

        return carry

    lax.fori_loop(0, PLANE, one_source, 0)
    for n in range(PLANE - 1):
        add(jnp.int32(n), rows_from(PLANE - 1))

    take_hop(3)

    src, low, ours = shard(jnp.int32(PLANE - 1))
    product = lax.dot_general(
        attn[...].reshape(PLANE * rows, attn.shape[2]), weights[src], NT,
        preferred_element_type=jnp.float32,
    ).astype(jnp.bfloat16).reshape(PLANE, rows, w_ref.shape[0])

    @pl.when(ours)
    def _():
        mine[low] = product

    @pl.when(jnp.logical_not(ours))
    def _():
        to_core[low] = product
        for t in range(PLANE):
            to_sibling(low, t).start()

    def last_sum(o, carry):
        add(jnp.int32(PLANE - 1), rows_from(PLANE - 1 - o))
        return carry

    lax.fori_loop(0, PLANE, last_sum, 0)

    for low in (0, 1):
        for t in range(PLANE):
            to_sibling(low, t).wait_send()

            @pl.when(t != i)
            def _():
                out_arrival(low, t).wait_recv()
                out_arrival(low, t).wait_send()

    for o in (1, 2, 3):
        for c in (0, 1):
            prefix_up(o, c).wait_send()
            prefix_across(o, c).wait_send()
            across_own_sent = across_own(o, c)

            @pl.when((i + o < PLANE) | (z >= 1))
            def _():
                across_own_sent.wait_send()
    for g in range(kv_heads):
        attn_to_x(g).wait_send()
        attn_to_y(g).wait_send()
        y_to_x(g).wait_send()
    for k in (1, 2, 3):
        for way in (0, 1):
            @pl.when(sends_hop(way, k))
            def _():
                weight_hop(way, k).wait_send()


def per_device_fused(
    queries,
    suffix_key_rows,
    suffix_value_rows,
    shared_prefix_keys,
    shared_prefix_values,
    out_weight,
    lengths,
):
    rows, q_cols = queries.shape
    kv_cols = suffix_key_rows.shape[1]
    columns = out_weight.shape[1]
    held = shared_prefix_keys.shape[0] * PLANE * PLANE + (REACH + 1) * rows
    kv_heads = kv_cols // HEAD_SIZE
    vmem = pl.BlockSpec(memory_space=pltpu.VMEM)
    low = jnp.bfloat16
    sem = pltpu.SemaphoreType.DMA
    blocks = pl.pallas_call(
        fused_kernel,
        out_shape=jax.ShapeDtypeStruct((2 * PLANE, rows, columns), low),
        in_specs=[pl.BlockSpec(memory_space=pl.ANY)] * 6 + [pl.BlockSpec(memory_space=pltpu.SMEM)],
        out_specs=vmem,
        scratch_shapes=[
            pltpu.VMEM((rows, q_cols), low),
            pltpu.VMEM((held, kv_cols), low),
            pltpu.VMEM((held, kv_cols), low),
            pltpu.VMEM((rows, (REACH + 1) * rows), jnp.float32),
            pltpu.VMEM((PLANE, columns, q_cols), low),
            pltpu.VMEM((PLANE, rows, q_cols), low),
            pltpu.VMEM((2, PLANE, rows, columns), low),
            pltpu.VMEM((2, PLANE, rows, columns), low),
            pltpu.VMEM((2, PLANE, rows, columns), low),
            pltpu.VMEM((2, PLANE, rows, columns), low),
            sem((6,)), sem((4, 2)), sem((4, 2)), sem((4, 2)), sem((4, 2)),
            sem((REACH + 1, 2)), sem((REACH + 1, 2)),
            sem((2, 4)), sem((2, 4)),
            sem((kv_heads, 3)), sem((kv_heads, 3)),
            sem((2, PLANE)), sem((2, PLANE)), sem((2, PLANE)), sem((2, PLANE)),
        ],
        compiler_params=pltpu.CompilerParams(
            collective_id=0, has_side_effects=True, vmem_limit_bytes=60 * 1024 * 1024
        ),
        cost_estimate=pl.CostEstimate(
            flops=12_000_000_000, bytes_accessed=8_000_000, transcendentals=10_000_000
        ),
    )(
        queries, suffix_key_rows, suffix_value_rows, shared_prefix_keys, shared_prefix_values,
        out_weight.T, lengths,
    )
    return jnp.transpose(blocks, (1, 0, 2)).reshape(rows, 2 * PLANE * columns)


def solution(mesh):
    fused = mesh.shape["mp"] == 2 and mesh.shape["blk"] == PLANE * PLANE
    placed = (
        P("blk", "mp"),
        P("blk", "mp"),
        P("blk", "mp"),
        P("blk", "mp"),
        P("blk", "mp"),
        P("mp", "blk"),
        P(),
    )
    return jax.shard_map(
        per_device_fused if fused else per_device, mesh=mesh, in_specs=placed, out_specs=P("blk", "mp"), check_vma=False
    )
```
